32 devices in a mesh: seq: 8 (over z, y), head: 4 (over x, core).
Axes of the slice: x: 2, y: 2, z: 4, core: 2. Of those that a mesh axis runs over, the one named last changes fastest.
Arguments:
- tokens: bfloat16 [2, 2048, 768], P(None, 'seq'), may hold values from -6 to 6
- norm_gain: float32 [768], replicated, may hold values from 0.5 to 1.5
- gate_proj: bfloat16 [768, 1536], P(None, 'head'), may hold values from -0.21875 to 0.21875
- value_proj: bfloat16 [768, 1536], P(None, 'head'), may hold values from -0.21875 to 0.21875
- state_proj: bfloat16 [768, 256], replicated, may hold values from -0.21875 to 0.21875
- step_proj: bfloat16 [768, 24], P(None, 'head'), may hold values from -0.21875 to 0.21875
- conv_value: float32 [4, 1536], P(None, 'head'), may hold values from -3 to 3
- conv_value_bias: float32 [1536], P('head'), may hold values from -3 to 3
- conv_state: float32 [4, 256], replicated, may hold values from -3 to 3
- conv_state_bias: float32 [256], replicated, may hold values from -3 to 3
- step_bias: float32 [24], P('head'), may hold values from -1 to 0.5
- decay_log: float32 [24], P('head'), may hold values from -9.2 to -3
- skip_gain: float32 [24], P('head'), may hold values from 0.5 to 1.5
- out_gain: float32 [1536], P('head'), may hold values from 0.5 to 1.5
- out_proj: bfloat16 [1536, 768], P('head'), may hold values from -0.15625 to 0.15625
- cotangent: float32 [2, 2048, 768], P(None, 'seq', 'head'), may hold values from -6 to 6
Outputs:
- mixed_rows: float32 [2, 2048, 768], P(None, 'seq', 'head')
- grad_tokens: float32 [2, 2048, 768], P(None, 'seq', 'head')
- grad_norm_gain: float32 [768], replicated
- grad_gate_proj: float32 [768, 1536], P(None, 'head')
- grad_value_proj: float32 [768, 1536], P(None, 'head')
- grad_state_proj: float32 [768, 256], replicated
- grad_step_proj: float32 [768, 24], P(None, 'head')
- grad_conv_value: float32 [4, 1536], P(None, 'head')
- grad_conv_value_bias: float32 [1536], P('head')
- grad_conv_state: float32 [4, 256], replicated
- grad_conv_state_bias: float32 [256], replicated
- grad_step_bias: float32 [24], P('head')
- grad_decay_log: float32 [24], P('head')
- grad_skip_gain: float32 [24], P('head')
- grad_out_gain: float32 [1536], P('head')
- grad_out_proj: float32 [1536, 768], P('head')
The draws below stay inside these ranges and needn't reach their ends.
All inputs are finite; a program needn't handle non-finite values.
Results may differ from the reference program's by a relative error of at most 0.0082.
Values may be sent and summed in bfloat16 or wider, within the bound.
No kernel may reach another device: no remote copies, remote signals or barrier semaphores. Data moves between devices by JAX's collectives and lax.ppermute only.
A program may use at most 128 MiB of HBM per device.

```python
import jax
import jax.numpy as jnp
from jax import lax

D = 768
HEADS = 24
HEAD_DIM = 64
NSTATE = 128
KCONV = 4
LEN_DEV = 256
SEQS = 2
DI = 1536
LENGTH = 2048


def levels(rng, dims, pieces, least, top_value):
    loudness = 1.0
    for axis_at, blocks in pieces:
        heights = jax.random.uniform(jax.random.fold_in(jax.random.fold_in(rng, 6), axis_at), (blocks,), jnp.float32, least / len(pieces), top_value / len(pieces))
        loudness = loudness * jnp.repeat(jnp.exp(heights), dims[axis_at] // blocks).reshape((-1,) + (1,) * (len(dims) - 1 - axis_at))
    return loudness


def gaussian(rng, extent, spread, reach, pieces=(), dtype=jnp.bfloat16):
    array = jax.random.normal(rng, extent, jnp.float32) * spread
    if len(pieces) > 0:
        array = levels(rng, extent, pieces, -0.22, 0.18) * array
    return jnp.clip(array, min=-reach, max=reach).astype(dtype)


def setup_inputs(seed: int = 0) -> dict:
    key_list = jax.random.split(jax.random.key(seed), 17)
    tokens = gaussian(key_list[0], (SEQS, LENGTH, D), 1.0, 6.0, ((1, 8),))
    norm_gain = jnp.clip(1.0 + 0.1 * jax.random.normal(key_list[1], (D,), jnp.float32), 0.5, 1.5)
    gate_proj = gaussian(key_list[2], (D, DI), D ** -0.5, 0.21875, ((1, 4),))
    value_proj = gaussian(key_list[3], (D, DI), D ** -0.5, 0.21875, ((1, 4),))
    state_proj = gaussian(key_list[4], (D, 2 * NSTATE), D ** -0.5, 0.21875)
    step_proj = gaussian(key_list[5], (D, HEADS), D ** -0.5, 0.21875, ((1, 4),))
    conv_value = gaussian(key_list[6], (KCONV, DI), 0.5, 3.0, ((1, 4),), jnp.float32)
    conv_value_bias = gaussian(key_list[7], (DI,), 0.5, 3.0, ((0, 4),), jnp.float32)
    conv_state = gaussian(key_list[8], (KCONV, 2 * NSTATE), 0.5, 3.0, (), jnp.float32)
    conv_state_bias = gaussian(key_list[9], (2 * NSTATE,), 0.5, 3.0, (), jnp.float32)
    step_bias = jnp.clip(-1.0 + 1.5 * jax.random.uniform(key_list[10], (HEADS,), jnp.float32) ** levels(key_list[10], (HEADS,), ((0, 4),), -0.2, 0.2), -1.0, 0.5)
    decay_log = jnp.clip(-9.2 + 6.2 * jax.random.uniform(key_list[11], (HEADS,), jnp.float32) ** levels(key_list[11], (HEADS,), ((0, 4),), -0.2, 0.2), -9.2, -3.0)
    skip_gain = jnp.clip(0.5 + 1.0 * jax.random.uniform(key_list[12], (HEADS,), jnp.float32) ** levels(key_list[12], (HEADS,), ((0, 4),), -0.2, 0.2), 0.5, 1.5)
    out_gain = jnp.clip(1.0 + 0.1 * jax.random.normal(key_list[13], (DI,), jnp.float32), 0.5, 1.5)
    out_proj = gaussian(key_list[14], (DI, D), DI ** -0.5, 0.15625, ((0, 4),))
    cotangent = gaussian(key_list[15], (SEQS, LENGTH, D), 1.0, 6.0, ((1, 8), (2, 4)), jnp.float32)
    return dict(tokens=tokens, norm_gain=norm_gain, gate_proj=gate_proj, value_proj=value_proj, state_proj=state_proj, step_proj=step_proj, conv_value=conv_value, conv_value_bias=conv_value_bias, conv_state=conv_state, conv_state_bias=conv_state_bias, step_bias=step_bias, decay_log=decay_log, skip_gain=skip_gain, out_gain=out_gain, out_proj=out_proj, cotangent=cotangent)


@jax.custom_vjp
def low(v):
    return lax.optimization_barrier(v.astype(jnp.bfloat16)).astype(jnp.float32)

@jax.custom_vjp
def low_back(v):
    return v

def low_keep(v):
    return (low(v), None)

def low_pass(kept, grad):
    return (grad,)

def back_keep(v):
    return (v, None)

def back_low(kept, grad):
    return (low(grad),)
low.defvjp(low_keep, low_pass)
low_back.defvjp(back_keep, back_low)
EPS = 1e-05
HIGHEST = lax.Precision.HIGHEST

def matmul(left, right):
    return jnp.dot(left, right, precision=HIGHEST, preferred_element_type=jnp.float32)

def block_step(carried, block_data):
    scaled, b_rows, c_rows, log_decay = block_data
    cumulative = jnp.cumsum(log_decay, axis=0)
    positions = jnp.arange(LEN_DEV)
    causal = positions[:, None] >= positions[None, :]
    cum_heads = cumulative.T
    differences = cum_heads[:, :, None] - cum_heads[:, None, :]
    decay_mat = jnp.exp(jnp.where(causal[None], differences, -1e+30))
    intersection = matmul(c_rows, b_rows.T)
    mix_mat = decay_mat * intersection[None]
    inside_sum = jnp.einsum('hij,jhp->ihp', mix_mat, scaled, precision=HIGHEST)
    state_read = jnp.einsum('hpn,in->ihp', carried, c_rows, precision=HIGHEST)
    carried_sum = jnp.exp(cumulative)[:, :, None] * state_read
    end_weights = jnp.exp(cumulative[-1][None, :] - cumulative)
    end_state = jnp.exp(cumulative[-1])[:, None, None] * carried + jnp.einsum('jh,jhp,jn->hpn', end_weights, scaled, b_rows, precision=HIGHEST)
    return (end_state, inside_sum + carried_sum)

def layer(source, norm_gain, gate_proj, value_proj, state_proj, step_proj, conv_value, conv_value_bias, conv_state, conv_state_bias, step_bias, decay_log, skip_gain, out_gain, out_proj):
    row_count = source.shape[0]
    rms_scale = lax.rsqrt(lax.optimization_barrier(jnp.mean(source * source, axis=-1, keepdims=True)) + EPS)
    normed = low(source * rms_scale * norm_gain)
    gate_pre = low_back(matmul(normed, gate_proj))
    value_pre = low_back(matmul(normed, value_proj))
    state_pre = low_back(matmul(normed, state_proj))
    step_pre = low_back(matmul(normed, step_proj))
    conv_in = jnp.concatenate([value_pre, state_pre], axis=-1)
    conv_weight = jnp.concatenate([conv_value, conv_state], axis=-1)
    conv_bias = jnp.concatenate([conv_value_bias, conv_state_bias], axis=-1)
    padded = jnp.pad(conv_in, ((KCONV - 1, 0), (0, 0)))
    conv_out = conv_bias[None, :] + jnp.zeros_like(conv_in)
    for kernel_tap in range(KCONV):
        conv_out = conv_out + conv_weight[kernel_tap][None, :] * padded[kernel_tap:kernel_tap + row_count]
    activated = jax.nn.silu(conv_out)
    values = activated[:, :DI].reshape(row_count, HEADS, HEAD_DIM)
    b_rows = activated[:, DI:DI + NSTATE]
    c_rows = activated[:, DI + NSTATE:]
    step_size = jax.nn.softplus(step_pre + step_bias)
    log_decay = -step_size * jnp.exp(decay_log)
    scaled = values * step_size[:, :, None]
    blocks = row_count // LEN_DEV
    initial = jnp.zeros((HEADS, HEAD_DIM, NSTATE), jnp.float32)
    last_state, outputs = lax.scan(jax.checkpoint(block_step), initial, (scaled.reshape(blocks, LEN_DEV, HEADS, HEAD_DIM), b_rows.reshape(blocks, LEN_DEV, NSTATE), c_rows.reshape(blocks, LEN_DEV, NSTATE), log_decay.reshape(blocks, LEN_DEV, HEADS)))
    scan_out = outputs.reshape(row_count, HEADS, HEAD_DIM) + skip_gain[None, :, None] * values
    gated = scan_out.reshape(row_count, DI) * jax.nn.silu(gate_pre)
    gate_scale = lax.rsqrt(lax.optimization_barrier(jnp.mean(gated * gated, axis=-1, keepdims=True)) + EPS)
    gate_low = low(gated * gate_scale * out_gain)
    branch = low_back(matmul(gate_low, out_proj))
    return source + branch

def reference(tokens, norm_gain, gate_proj, value_proj, state_proj, step_proj, conv_value, conv_value_bias, conv_state, conv_state_bias, step_bias, decay_log, skip_gain, out_gain, out_proj, cotangent):
    params = tuple((param.astype(jnp.float32) for param in (norm_gain, gate_proj, value_proj, state_proj, step_proj, conv_value, conv_value_bias, conv_state, conv_state_bias, step_bias, decay_log, skip_gain, out_gain, out_proj)))

    def one_sequence(totals, sequence_pair):
        source, grad_output = sequence_pair
        mixed_rows, pullback = jax.vjp(layer, source, *params)
        gradients = pullback(grad_output)
        totals = tuple((first + second for first, second in zip(totals, gradients[1:])))
        return (totals, (mixed_rows, gradients[0]))
    initial = tuple((jnp.zeros_like(param) for param in params))
    totals, (mixed_rows, grad_tokens) = lax.scan(one_sequence, initial, (tokens.astype(jnp.float32), cotangent))
    return (mixed_rows, grad_tokens, totals[0], totals[1], totals[2], totals[3], totals[4], totals[5], totals[6], totals[7], totals[8], totals[9], totals[10], totals[11], totals[12], totals[13])
```

```python
import functools

import jax
import jax.numpy as jnp
from jax import lax
from jax.experimental import pallas as pl
from jax.experimental.pallas import tpu as pltpu
from jax.sharding import PartitionSpec as P

EPS = 1e-05
F32 = jnp.float32
BF16 = jnp.bfloat16
NN = ((1,), (0,))
NT = ((1,), (1,))
TN = ((0,), (0,))
PAD = 16
LANES = 128


def shift(x, axis, by):
    devices = lax.axis_size(axis)
    pairs = [(i, i + by) for i in range(devices) if 0 <= i + by < devices]
    return lax.ppermute(x, axis, pairs)


def swap(x, axis, mask):
    devices = lax.axis_size(axis)
    return lax.ppermute(x, axis, [(i, i ^ mask) for i in range(devices)])


def masks(axis):
    found, mask = [], 1
    while mask < lax.axis_size(axis):
        found.append(mask)
        mask *= 2
    return found


def sum_all(x, axis):
    for mask in masks(axis):
        x = x + swap(x, axis, mask)
    return x


def orders(axis_size):
    near = [1 << t for t in range(axis_size.bit_length() - 1)]
    return near, near[1:2] + near[:1] + near[2:]


def places(order):
    bits = len(order)
    return [
        sum(((p >> (bits - 1 - t)) & 1) * order[t] for t in range(bits))
        for p in range(1 << bits)
    ]


def add_wide(left, right):
    return (left.astype(F32) + right.astype(F32)).astype(left.dtype)


class Reduce:
    def __init__(self, keep, send, axis, order):
        self.keep, self.send, self.axis, self.order = keep, send, axis, list(order)

    def step(self, after=()):
        got = swap(self.send, self.axis, self.order.pop(0))
        got = lax.optimization_barrier((got, after))[0]
        half = self.keep.shape[0] // 2
        if half == 0:
            self.keep, self.send = add_wide(self.keep[0], got[0]), None
        else:
            self.send = add_wide(self.keep[half:], got[half:])
            self.keep = add_wide(self.keep[:half], got[:half])

    def finish(self):
        while self.order:
            self.step()
        return self.keep


class Gather:
    def __init__(self, x, axis, order):
        self.near, self.far, self.axis, self.order = x[None], None, axis, list(order)

    def step(self):
        if self.far is not None:
            self.near = jnp.concatenate([self.near, self.far], axis=0)
        self.far = swap(self.near, self.axis, self.order.pop())

    def finish(self):
        while self.order:
            self.step()
        return self.near, self.far


def hold(x, *chains):
    held = [(c.keep, c.send) if isinstance(c, Reduce) else (c.near, c.far) for c in chains]
    x, held = lax.optimization_barrier((x, held))
    for chain, state in zip(chains, held):
        if isinstance(chain, Reduce):
            chain.keep, chain.send = state
        else:
            chain.near, chain.far = state
    return x


def dot(left, right, dims=NN):
    return lax.dot_general(left, right, (dims, ((), ())), preferred_element_type=F32)


def parts(x, count):
    found = []
    for _ in range(count):
        term = x.astype(BF16)
        found.append(term)
        x = x - term.astype(F32)
    return found


def dot_fine(left, right, dims=NN):
    left_high, left_low = parts(left, 2)
    right_high, right_low = parts(right, 2)
    return (
        dot(left_high, right_high, dims)
        + dot(left_low, right_high, dims)
        + dot(left_high, right_low, dims)
    )


def dot_left(left, right, dims=NN, count=2):
    return sum(dot(term, right, dims) for term in parts(left, count))


def dot_right(left, right, dims=NN, count=2):
    return sum(dot(left, term, dims) for term in parts(right, count))


def silu(x):
    return x * jax.nn.sigmoid(x)


def silu_slope(inputs):
    sigma = jax.nn.sigmoid(inputs)
    return sigma * (1.0 + inputs * (1.0 - sigma))


def softplus(x):
    return jnp.maximum(x, 0.0) + jnp.log1p(jnp.exp(-jnp.abs(x)))


def iota(shape, dim):
    return lax.broadcasted_iota(jnp.int32, shape, dim)


def spread(heads, inner):
    lane, head = iota((heads, inner), 1), iota((heads, inner), 0)
    size = inner // heads
    inside = (lane >= head * size) & (lane < (head + 1) * size)
    return jnp.where(inside, 1.0, 0.0).astype(BF16)


def lane_blocks(heads, inner):
    size = inner // heads
    for start in range(0, inner, LANES):
        stop = min(start + LANES, inner)
        yield start, stop, range(start // size, stop // size)


def head_lanes(start, stop, head, size, length):
    lane = iota((length, stop - start), 1) + start
    return (lane >= head * size) & (lane < (head + 1) * size)


def local(body, outs, args, scratch=(), steps=1, flops=100_000_000):
    def spec(shape, dim, smem=False):
        if smem:
            return pl.BlockSpec(memory_space=pltpu.SMEM)
        block = [size // steps if at == dim else size for at, size in enumerate(shape)]
        return pl.BlockSpec(
            tuple(block),
            lambda step, dim=dim: tuple(step if at == dim else 0 for at in range(len(shape))),
        )

    pairs = [a if isinstance(a, tuple) else (a, None) for a in args]
    trio = [o if len(o) == 3 else (*o, None) for o in outs]
    size = sum(a.size * a.dtype.itemsize for a, _ in pairs)
    return pl.pallas_call(
        body,
        grid=(steps,),
        out_shape=[jax.ShapeDtypeStruct(shape, dtype) for shape, dtype, _ in trio],
        in_specs=[spec(a.shape, dim, a.dtype == jnp.int32) for a, dim in pairs],
        out_specs=[spec(shape, dim) for shape, _, dim in trio],
        scratch_shapes=list(scratch),
        compiler_params=pltpu.CompilerParams(vmem_limit_bytes=60 * 2**20),
        cost_estimate=pl.CostEstimate(
            flops=flops, bytes_accessed=size // 4, transcendentals=0
        ),
    )(*[a for a, _ in pairs])


def accumulate(ref, value):
    first = pl.program_id(0) == 0

    @pl.when(first)
    def _():
        ref[...] = value

    @pl.when(jnp.logical_not(first))
    def _():
        ref[...] += value


def as_row(ref):
    return ref[...].reshape(1, -1)


def as_column(row):
    count = row.shape[1]
    eye = iota((count, count), 0) == iota((count, count), 1)
    return jnp.sum(jnp.where(eye, row, 0.0), axis=1, keepdims=True)


def first_kernel(
    tokens_ref,
    edge_ref,
    gain_ref,
    value_proj_ref,
    state_proj_ref,
    step_proj_ref,
    conv_value_ref,
    conv_value_bias_ref,
    conv_state_ref,
    conv_state_bias_ref,
    step_bias_ref,
    decay_log_ref,
    normed_ref,
    value_in_ref,
    state_in_ref,
    values_ref,
    states_ref,
    value_slope_ref,
    state_slope_ref,
    step_x_ref,
    exp_cum_x_ref,
    end_x_ref,
    cum_ref,
    cum_t_ref,
    step_arg_t_ref,
    ends_ref,
):
    _, length, _ = tokens_ref.shape
    inner = values_ref.shape[2]
    heads = cum_ref.shape[2]
    nstate = states_ref.shape[2] // 2
    blocks, share = ends_ref.shape[0], ends_ref.shape[1] - 8
    spread_mat = spread(heads, inner)
    row, col = iota((length, length), 0), iota((length, length), 1)
    lower = jnp.where(row >= col, 1.0, 0.0).astype(BF16)
    upper = jnp.where(row <= col, 1.0, 0.0).astype(BF16)
    step_bias = as_row(step_bias_ref)
    rate = jnp.exp(as_row(decay_log_ref))
    for source, first, count in ((edge_ref, 0, PAD), (tokens_ref, PAD, length)):
        x = source[0].astype(F32)
        scale = lax.rsqrt(jnp.mean(x * x, axis=-1, keepdims=True) + EPS)
        normed_ref[0, first : first + count] = (x * scale * as_row(gain_ref)).astype(BF16)
    normed = normed_ref[0, PAD:]
    step_arg = dot(normed, step_proj_ref[...], NT) + step_bias
    step_arg_t = dot(step_proj_ref[...], normed, NT) + as_column(step_bias)
    step_arg_t_ref[0] = step_arg_t
    step = softplus(step_arg)
    cum = dot_right(lower, -step * rate, NN, 3)
    cum_ref[0] = cum
    cum_t_ref[0] = dot_left(-softplus(step_arg_t) * as_column(rate), upper, NN, 3)
    step_x = dot_left(step, spread_mat)
    exp_cum_x = dot_left(jnp.exp(cum), spread_mat)
    end_x = dot_left(jnp.exp(cum[length - 1 :] - cum), spread_mat)
    step_x_ref[0] = step_x
    exp_cum_x_ref[0] = exp_cum_x
    end_x_ref[0] = end_x

    def convolve(proj_ref, weight_ref, bias_ref, in_ref, out_ref, slope_ref):
        taps = weight_ref.shape[0]
        in_ref[0] = dot(normed_ref[0], proj_ref[...])
        conv_out = as_row(bias_ref)
        for tap in range(taps):
            first = PAD - taps + 1 + tap
            conv_out = conv_out + weight_ref[tap : tap + 1] * in_ref[0, first : first + length]
        sigma = jax.nn.sigmoid(conv_out)
        slope_ref[0] = sigma * (1.0 + conv_out * (1.0 - sigma))
        out_ref[0] = conv_out * sigma

    convolve(
        state_proj_ref,
        conv_state_ref,
        conv_state_bias_ref,
        state_in_ref,
        states_ref,
        state_slope_ref,
    )
    convolve(
        value_proj_ref,
        conv_value_ref,
        conv_value_bias_ref,
        value_in_ref,
        values_ref,
        value_slope_ref,
    )
    ends = dot_fine(states_ref[0, :, :nstate], end_x * step_x * values_ref[0], TN)
    for block in range(blocks):
        ends_ref[block, 0:8] = jnp.broadcast_to(exp_cum_x[length - 1 :], (8, inner))
        ends_ref[block, 8:] = ends[block * share : (block + 1) * share]


def scan_kernel(got_ref, entering_ref):
    running = jnp.zeros(entering_ref.shape[1:], F32)
    for block in range(got_ref.shape[0]):
        entering_ref[block] = running
        running = got_ref[block, 0:1] * running + got_ref[block, 8:]


def back_scan_kernel(got_ref, back_ref, leaving_ref):
    running = jnp.zeros(leaving_ref.shape[1:], F32)
    for block in reversed(range(got_ref.shape[0])):
        leaving_ref[block] = running
        running = got_ref[block, 0:1] * running + back_ref[block]


def inside_kernel(
    normed_ref,
    gate_proj_ref,
    values_ref,
    states_ref,
    step_x_ref,
    cum_ref,
    cum_t_ref,
    cot_ref,
    out_proj_ref,
    skip_ref,
    base_ref,
    gnorm_ref,
    gate_pre_ref,
):
    seqs, length, inner = base_ref.shape
    heads = cum_ref.shape[2]
    size = inner // heads
    nstate = states_ref.shape[2] // 2
    skip = dot_left(as_row(skip_ref), spread(heads, inner), NN, 3)
    causal = iota((length, length), 0) >= iota((length, length), 1)
    for seq in range(seqs):
        gate_pre_ref[seq] = dot(normed_ref[seq, PAD:], gate_proj_ref[...])
        products = dot_fine(states_ref[seq, :, nstate:], states_ref[seq, :, :nstate], NT)
        for start, stop, block_heads in lane_blocks(heads, inner):
            values = values_ref[seq, :, start:stop]
            scaled = parts(values * step_x_ref[seq, :, start:stop], 2)
            total = None
            for head in block_heads:
                gap = cum_ref[seq, :, head : head + 1] - cum_t_ref[seq, head : head + 1, :]
                decay = jnp.exp(jnp.where(causal, gap, -1e30))
                high, low = parts(decay * products, 2)
                part = dot(high, scaled[0]) + dot(low, scaled[0]) + dot(high, scaled[1])
                if total is None:
                    total = part
                else:
                    total = jnp.where(head_lanes(start, stop, head, size, length), part, total)
            base_ref[seq, :, start:stop] = total + skip[:, start:stop] * values
        gnorm_ref[seq] = dot(cot_ref[seq * length : (seq + 1) * length], out_proj_ref[...], NT)


def read_kernel(
    state_ref,
    states_ref,
    exp_cum_x_ref,
    base_ref,
    gate_pre_ref,
    gnorm_ref,
    out_gain_ref,
    read_ref,
    sums_ref,
):
    seqs, length, inner = base_ref.shape
    nstate = states_ref.shape[2] // 2
    ones = jnp.ones((8, inner), BF16)
    for seq in range(seqs):
        read = exp_cum_x_ref[seq] * dot_fine(states_ref[seq, :, nstate:], state_ref[seq])
        read_ref[seq] = read
        gated = (base_ref[seq] + read) * silu(gate_pre_ref[seq])
        squares = dot_right(ones, gated * gated, NT)
        backs = dot_right(ones, gnorm_ref[seq] * as_row(out_gain_ref) * gated, NT)
        row = iota((8, length), 0)
        sums_ref[:, seq * length : (seq + 1) * length] = jnp.where(row == 0, squares, backs)


def gate_kernel(
    sums_ref,
    read_ref,
    base_ref,
    gate_pre_ref,
    gnorm_ref,
    out_gain_ref,
    exp_cum_x_ref,
    states_ref,
    grad_scan_ref,
    back_ref,
    *,
    inner_total,
):
    nstate = states_ref.shape[2] // 2
    blocks, share = back_ref.shape[0], back_ref.shape[1]
    sums = jnp.transpose(sums_ref[...])
    scale = lax.rsqrt(sums[:, 0:1] / inner_total + EPS)
    back_mean = scale * sums[:, 1:2] / inner_total
    gate_act = silu(gate_pre_ref[0])
    unit = (base_ref[0] + read_ref[0]) * gate_act * scale
    grad_gated = scale * (gnorm_ref[0] * as_row(out_gain_ref) - unit * back_mean)
    grad_scan = grad_gated * gate_act
    grad_scan_ref[0] = grad_scan
    back = dot_fine(states_ref[0, :, nstate:], exp_cum_x_ref[0] * grad_scan, TN)
    for block in range(blocks):
        back_ref[block] = back[block * share : (block + 1) * share]


def cut_lines(held, value):
    count = held.shape[1]
    for piece in range(held.shape[0]):
        held[piece] = value[piece * count : (piece + 1) * count]


def stacked(lines, lanes):
    return [lines[:, at : at + lanes] for at in range(0, lines.shape[1], lanes)]


def ordered_piece(own, at, value, keep_ref, send_ref):
    half = keep_ref.shape[0]
    for p, mask in enumerate(places(orders(2 * half)[0])):

        @pl.when((own ^ mask) == at)
        def _():
            (keep_ref if p < half else send_ref)[p % half] = value


def low_kernel(
    own_ref,
    sums_ref,
    read_ref,
    base_ref,
    gate_pre_ref,
    gnorm_ref,
    out_gain_ref,
    grad_scan_ref,
    values_ref,
    normed_ref,
    cot_ref,
    out_proj_ref,
    grad_gate_ref,
    rows_ref,
    keep_ref,
    send_ref,
    branch_keep_ref,
    branch_send_ref,
    gate_low,
    grad_gate_proj,
    grad_out_proj,
    *,
    inner_total,
):
    seqs, length, inner = base_ref.shape
    gain_sum = jnp.zeros((1, inner), F32)
    skip_sum = jnp.zeros((1, inner), F32)
    pieces = 2 * branch_keep_ref.shape[0]
    col_width = branch_keep_ref.shape[2]
    total = None
    for seq in range(seqs):
        sums = jnp.transpose(sums_ref[:, seq * length : (seq + 1) * length])
        scale = lax.rsqrt(sums[:, 0:1] / inner_total + EPS)
        back_mean = scale * sums[:, 1:2] / inner_total
        gate_pre = gate_pre_ref[seq]
        sigma = jax.nn.sigmoid(gate_pre)
        scan_out = base_ref[seq] + read_ref[seq]
        unit = scan_out * gate_pre * sigma * scale
        gnorm = gnorm_ref[seq]
        gate_low[seq * length : (seq + 1) * length] = (unit * as_row(out_gain_ref)).astype(BF16)
        grad_gated = scale * (gnorm * as_row(out_gain_ref) - unit * back_mean)
        slope = sigma * (1.0 + gate_pre * (1.0 - sigma))
        grad_gate = (grad_gated * scan_out * slope).astype(BF16)
        grad_gate_ref[seq] = grad_gate
        part = dot(normed_ref[seq, PAD:], grad_gate, TN)
        total = part if total is None else total + part
        gain_sum = gain_sum + jnp.sum(gnorm * unit, axis=0, keepdims=True)
        skip_sum = skip_sum + jnp.sum(
            grad_scan_ref[seq] * values_ref[seq], axis=0, keepdims=True
        )
    rows_ref[:, :inner] = gain_sum
    rows_ref[:, inner:] = skip_sum
    cut_lines(grad_gate_proj, total)
    cut_lines(grad_out_proj, dot(gate_low[...], cot_ref[...], TN))
    blocks = 2 * keep_ref.shape[0]
    for p, mask in enumerate(places(orders(blocks)[0])):
        at = own_ref[0] ^ mask
        ref = keep_ref if p < blocks // 2 else send_ref
        value = jnp.concatenate(
            [grad_gate_proj[at], *stacked(grad_out_proj[at], inner)], axis=0
        )
        ref[p % (blocks // 2)] = value.astype(BF16)
    branch = dot(gate_low[...], out_proj_ref[...])
    for piece in range(pieces):
        value = branch[:, piece * col_width : (piece + 1) * col_width].astype(BF16)
        ordered_piece(own_ref[1], piece, value, branch_keep_ref, branch_send_ref)


def mix_kernel(
    values_ref,
    states_ref,
    step_x_ref,
    exp_cum_x_ref,
    cum_ref,
    cum_t_ref,
    grad_scan_ref,
    state_ref,
    scaled_grad_ref,
    grad_b_ref,
    grad_c_ref,
    gaps_ref,
):
    seqs, length, inner = grad_scan_ref.shape
    heads = cum_ref.shape[2]
    size = inner // heads
    nstate = states_ref.shape[2] // 2
    causal = iota((length, length), 0) >= iota((length, length), 1)
    ones = jnp.ones((8, length), BF16)
    for seq in range(seqs):
        b_rows = states_ref[seq, :, :nstate]
        c_rows = states_ref[seq, :, nstate:]
        products = dot_fine(c_rows, b_rows, NT)
        grad_products = jnp.zeros((length, length), F32)
        for start, stop, block_heads in lane_blocks(heads, inner):
            scaled = values_ref[seq, :, start:stop] * step_x_ref[seq, :, start:stop]
            scaled_high, scaled_low = parts(scaled, 2)
            scan_high, scan_low = parts(grad_scan_ref[seq, :, start:stop], 2)
            total = None
            for head in block_heads:
                gap = cum_ref[seq, :, head : head + 1] - cum_t_ref[seq, head : head + 1, :]
                decay = jnp.exp(jnp.where(causal, gap, -1e30))
                own = head_lanes(start, stop, head, size, length)
                own_high = jnp.where(own, scan_high, jnp.zeros_like(scan_high))
                own_low = jnp.where(own, scan_low, jnp.zeros_like(scan_low))
                grad_mix = (
                    dot(own_high, scaled_high, NT)
                    + dot(own_low, scaled_high, NT)
                    + dot(own_high, scaled_low, NT)
                )
                grad_decayed = grad_mix * decay
                grad_products = grad_products + grad_decayed
                related = (grad_decayed * products).astype(BF16)
                gaps = dot(ones, related, NT) - dot(ones, related)
                gaps_ref[seq, head : head + 1] = gaps[0:1]
                part = dot((decay * products).astype(BF16), own_high, TN)
                total = part if total is None else total + part
            scaled_grad_ref[seq, :, start:stop] = total
        carried = exp_cum_x_ref[seq] * grad_scan_ref[seq]
        grad_c_ref[seq] = dot_fine(grad_products, b_rows) + dot_fine(
            carried, state_ref[seq], NT
        )
        grad_b_ref[seq] = dot_fine(grad_products, c_rows, TN)


def state_sum_kernel(
    own_ref,
    grad_end_ref,
    values_ref,
    step_x_ref,
    end_x_ref,
    grad_b_ref,
    grad_c_ref,
    keep_ref,
    send_ref,
):
    pieces, part = 2 * keep_ref.shape[0], keep_ref.shape[2]
    weighted = end_x_ref[0] * step_x_ref[0] * values_ref[0]
    grad_b = grad_b_ref[0] + dot_fine(weighted, grad_end_ref[0], NT)
    both = jnp.concatenate([grad_b, grad_c_ref[0]], axis=1)
    for piece in range(pieces):
        value = both[:, piece * part : (piece + 1) * part]
        ordered_piece(own_ref[1], piece, value, keep_ref, send_ref)


def conv_back(grad_out, in_ref, weight_ref, seq, around):
    length = grad_out.shape[0]
    taps = weight_ref.shape[0]
    around[PAD : PAD + length] = grad_out
    grad_in = None
    sums = []
    for tap in range(taps):
        first = PAD - taps + 1 + tap
        sums.append(
            jnp.sum(grad_out * in_ref[seq, first : first + length], axis=0, keepdims=True)
        )
        first = taps - 1 - tap
        part = weight_ref[tap : tap + 1] * around[first : first + PAD + length]
        grad_in = part if grad_in is None else grad_in + part
    sums.append(jnp.sum(grad_out, axis=0, keepdims=True))
    return grad_in, jnp.concatenate(sums, axis=0)


def clear_edges(around):
    zeros = jnp.zeros((PAD, around.shape[1]), F32)
    around[0:PAD] = zeros
    around[around.shape[0] - PAD :] = zeros


def value_kernel(
    grad_end_ref,
    state_ref,
    values_ref,
    states_ref,
    slope_ref,
    conv_in_ref,
    conv_weight_ref,
    step_x_ref,
    exp_cum_x_ref,
    end_x_ref,
    step_arg_t_ref,
    decay_log_ref,
    skip_ref,
    read_ref,
    grad_scan_ref,
    scaled_grad_ref,
    gaps_ref,
    grad_in_ref,
    grad_step_t_ref,
    conv_rows_ref,
    head_rows_ref,
    around,
):
    _, length, inner = values_ref.shape
    heads = gaps_ref.shape[1]
    nstate = states_ref.shape[2] // 2
    spread_mat = spread(heads, inner)
    row, col = iota((length, length), 0), iota((length, length), 1)
    lower = jnp.where(row >= col, 1.0, 0.0).astype(BF16)
    rate_t = as_column(jnp.exp(as_row(decay_log_ref)))
    skip = dot_left(as_row(skip_ref), spread_mat, NN, 3)
    last = iota((heads, length), 1) == length - 1
    clear_edges(around)
    values = values_ref[0]
    grad_end = grad_end_ref[0]
    step_x = step_x_ref[0]
    grad_scan = grad_scan_ref[0]
    end_proj = end_x_ref[0] * dot(
        states_ref[0, :, :nstate].astype(BF16), grad_end.astype(BF16)
    )
    scaled_grad = scaled_grad_ref[0] + end_proj
    grad_in, conv_rows = conv_back(
        (skip * grad_scan + step_x * scaled_grad) * slope_ref[0],
        conv_in_ref,
        conv_weight_ref,
        0,
        around,
    )
    grad_in_ref[0] = grad_in
    end_terms = dot_right(spread_mat, step_x * values * end_proj, NT)
    crossed = jnp.sum(grad_end * state_ref[0], axis=0, keepdims=True)
    crossed = crossed * exp_cum_x_ref[0, length - 1 :]
    last_term = jnp.sum(end_terms, axis=1, keepdims=True) + jnp.sum(
        jnp.where(spread_mat.astype(F32) > 0.0, crossed, 0.0), axis=1, keepdims=True
    )
    grad_cum = (
        gaps_ref[0] + dot_right(spread_mat, grad_scan * read_ref[0], NT) - end_terms
    ) + jnp.where(last, last_term, 0.0)
    grad_log = dot_left(grad_cum, lower, NN, 3)
    step_arg = step_arg_t_ref[0]
    rate_sum = -jnp.sum(grad_log * softplus(step_arg), axis=1, keepdims=True)
    grad_step = dot_right(spread_mat, values * scaled_grad, NT) - grad_log * rate_t
    grad_step = grad_step * jax.nn.sigmoid(step_arg)
    bias_sum = jnp.sum(grad_step, axis=1, keepdims=True)
    grad_step_t_ref[0] = grad_step.astype(BF16)
    lane = iota((heads, LANES), 1)
    accumulate(conv_rows_ref, conv_rows)
    accumulate(head_rows_ref, jnp.where(lane == 0, bias_sum, rate_sum * rate_t))


def weight_kernel(
    normed_ref,
    value_in_ref,
    grad_step_t_ref,
    state_grad_ref,
    slope_ref,
    conv_in_ref,
    conv_weight_ref,
    state_in_ref,
    conv_rows_ref,
    step_rows_ref,
    late_ref,
    around,
):
    seqs, length, _ = slope_ref.shape
    width = normed_ref.shape[2]
    blocks, _, inner = late_ref.shape
    value_total = state_total = step_total = conv_total = None

    def add(total, part):
        return part if total is None else total + part

    clear_edges(around)
    for seq in range(seqs):
        normed = normed_ref[seq]
        grad = state_grad_ref[seq * length : (seq + 1) * length] * slope_ref[seq]
        grad_in, conv_rows = conv_back(grad, conv_in_ref, conv_weight_ref, seq, around)
        state_in_ref[seq] = grad_in
        conv_total = add(conv_total, conv_rows)
        value_total = add(value_total, dot(normed, value_in_ref[seq].astype(BF16), TN))
        state_total = add(state_total, dot(grad_in.astype(BF16), normed, TN))
        step_total = add(step_total, dot(grad_step_t_ref[seq], normed_ref[seq, PAD:]))
    conv_rows_ref[...] = conv_total
    step_rows_ref[...] = step_total
    value_lines = width // blocks
    state_lines = state_total.shape[0] // blocks
    for block in range(blocks):
        value = value_total[block * value_lines : (block + 1) * value_lines]
        state = state_total[block * state_lines : (block + 1) * state_lines]
        value = jnp.concatenate([value, *stacked(state, inner)], axis=0)
        late_ref[block] = value.astype(BF16)


def sum_kernel(got_ref, value_ref, state_ref):
    total = got_ref[0].astype(F32)
    for block in range(1, got_ref.shape[0]):
        total = total + got_ref[block].astype(F32)
    total = total.astype(BF16)
    lines = value_ref.shape[1]
    for block in range(value_ref.shape[0]):
        value_ref[block] = total[:lines]
    state_ref[...] = total[lines:]


def place_kernel(own_ref, near_ref, far_ref, gate_ref, out_ref):
    blocks, lines, inner = gate_ref.shape
    count = out_ref.shape[1]
    for p, mask in enumerate(places(orders(blocks)[0])):
        ref = near_ref if p < blocks // 2 else far_ref
        value = ref[p % (blocks // 2)].astype(F32)
        at = own_ref[0] ^ mask
        gate_ref[at] = value[:lines]
        for group in range(out_ref.shape[2] // inner):
            first = lines + group * count
            out_ref[at, :, group * inner : (group + 1) * inner] = value[first : first + count]


def place_state_kernel(own_ref, near_ref, far_ref, out_ref, held):
    half, pieces, _, inner = near_ref.shape
    _, each, width = held.shape
    for p, mask in enumerate(places(orders(2 * half)[0])):
        ref = near_ref if p < half else far_ref
        for q, head_mask in enumerate(places(orders(pieces)[0])):
            value = ref[p % half, q].astype(F32)
            at = (own_ref[1] ^ head_mask) * 2 * half + (own_ref[0] ^ mask)
            for group in range(width // inner):
                held[at, :, group * inner : (group + 1) * inner] = value[
                    group * each : (group + 1) * each
                ]
    out_ref[...] = jnp.transpose(held[...].reshape(-1, width))


def back_kernel(
    own_ref,
    tokens_ref,
    gain_ref,
    value_in_ref,
    state_in_ref,
    value_over_ref,
    state_over_ref,
    value_proj_ref,
    state_proj_ref,
    grad_gate_ref,
    gate_proj_ref,
    grad_step_t_ref,
    step_proj_t_ref,
    keep_ref,
    send_ref,
    sums_ref,
    gain_sum_ref,
):
    _, length, width = tokens_ref.shape
    pieces, col_width = 2 * keep_ref.shape[0], keep_ref.shape[2]
    ones = jnp.ones((8, width), BF16)
    def whole(in_ref, over_ref, seq):
        return jnp.concatenate(
            [
                in_ref[seq, PAD:length].astype(BF16),
                (in_ref[seq, length:] + over_ref[seq]).astype(BF16),
            ],
            axis=0,
        )

    x = tokens_ref[0].astype(F32)
    unit = x * lax.rsqrt(jnp.mean(x * x, axis=-1, keepdims=True) + EPS)
    normed_grad = (
        dot(whole(value_in_ref, value_over_ref, 0), value_proj_ref[...], NT)
        + dot(whole(state_in_ref, state_over_ref, 0), state_proj_ref[...], NT)
        + dot(grad_gate_ref[0], gate_proj_ref[...], NT)
        + dot(grad_step_t_ref[0], step_proj_t_ref[...], TN)
    )
    accumulate(gain_sum_ref, jnp.sum(normed_grad * unit, axis=0, keepdims=True))
    unit_grad = normed_grad * as_row(gain_ref)
    sums_ref[...] = dot_right(ones, unit_grad * unit, NT)
    for piece in range(pieces):
        value = unit_grad[:, piece * col_width : (piece + 1) * col_width].astype(BF16)
        ordered_piece(own_ref[1], piece, value, keep_ref, send_ref)


def on_device(
    tokens,
    norm_gain,
    gate_proj,
    value_proj,
    state_proj,
    step_proj,
    conv_value,
    conv_value_bias,
    conv_state,
    conv_state_bias,
    step_bias,
    decay_log,
    skip_gain,
    out_gain,
    out_proj,
    cotangent,
):
    seqs, length, width = tokens.shape
    rows = seqs * length
    heads = step_proj.shape[1]
    inner = gate_proj.shape[1]
    head_dim = inner // heads
    nstate = state_proj.shape[1] // 2
    taps = conv_value.shape[0]
    channels = inner + 2 * nstate
    head_devices = lax.axis_size("head")
    blocks = lax.axis_size("seq")
    head_index = lax.axis_index("head")
    own = jnp.stack([lax.axis_index("seq"), head_index]).astype(jnp.int32)
    col_width = width // head_devices
    share = seqs * nstate // blocks
    part = 2 * nstate // head_devices
    full = (seqs, length, inner)
    inner_total = inner * head_devices

    def own_cols(x, size):
        return lax.dynamic_slice_in_dim(x, head_index * size, size, x.ndim - 1)

    def cut(*arrays):
        return [(x, 0) for x in arrays]

    edge_tokens = shift(tokens[:, length - PAD :, :], "seq", 1)
    step_proj_t = jnp.transpose(step_proj)
    (
        normed,
        value_conv_in,
        state_conv_in,
        values,
        states,
        value_slope,
        state_slope,
        step_x,
        exp_cum_x,
        end_x,
        cum,
        cum_t,
        step_arg_t,
        ends,
    ) = local(
        first_kernel,
        [
            ((seqs, PAD + length, width), BF16, 0),
            ((seqs, PAD + length, inner), F32, 0),
            ((seqs, PAD + length, 2 * nstate), F32, 0),
            (full, F32, 0),
            ((seqs, length, 2 * nstate), F32, 0),
            (full, F32, 0),
            ((seqs, length, 2 * nstate), F32, 0),
            (full, F32, 0),
            (full, F32, 0),
            (full, F32, 0),
            ((seqs, length, heads), F32, 0),
            ((seqs, heads, length), F32, 0),
            ((seqs, heads, length), F32, 0),
            ((blocks, 8 + share, inner), F32, 0),
        ],
        [
            *cut(tokens, edge_tokens),
            norm_gain,
            value_proj,
            state_proj,
            step_proj_t,
            conv_value,
            conv_value_bias,
            conv_state,
            conv_state_bias,
            step_bias,
            decay_log,
        ],
        steps=seqs,
    )
    got = lax.all_to_all(ends, "seq", 0, 0)
    cot_rows = cotangent.reshape(rows, col_width)
    cot_low, _ = lax.optimization_barrier((cot_rows.astype(BF16), ends))
    cot_low = lax.all_gather(cot_low, "head", axis=1, tiled=True)
    got, cot_low = lax.optimization_barrier((got, cot_low))
    (entering,) = local(scan_kernel, [((blocks, share, inner), F32)], [got])
    state_in = lax.all_to_all(entering, "seq", 0, 0).reshape(seqs, nstate, inner)
    base, gnorm, gate_pre = local(
        inside_kernel,
        [(full, F32, 0), (full, F32, 0), (full, F32, 0)],
        [
            (normed, 0),
            gate_proj,
            *cut(values, states, step_x, cum, cum_t, cot_low),
            out_proj,
            skip_gain,
        ],
        steps=seqs,
    )
    read, row_sums = local(
        read_kernel,
        [(full, F32, 0), ((8, rows), F32, 1)],
        [*cut(state_in, states, exp_cum_x, base, gate_pre, gnorm), out_gain],
        steps=seqs,
    )
    row_sums = sum_all(row_sums, "head")
    grad_scan, back = local(
        functools.partial(gate_kernel, inner_total=inner_total),
        [(full, F32, 0), ((blocks, share, inner), F32, 0)],
        [
            (row_sums, 1),
            *cut(read, base, gate_pre, gnorm),
            out_gain,
            *cut(exp_cum_x, states),
        ],
        steps=seqs,
    )
    got_back = lax.all_to_all(back, "seq", 0, 0)

    def halves(axis_size, lines, lanes, dtype=BF16, dim=None):
        return [((axis_size // 2, lines, lanes), dtype, dim)] * 2

    (
        grad_gate,
        inner_row,
        early_keep,
        early_send,
        branch_keep,
        branch_send,
    ) = local(
        functools.partial(low_kernel, inner_total=inner_total),
        [
            (full, BF16),
            ((1, 2 * inner), F32),
            *halves(blocks, 2 * (width // blocks), inner),
            *halves(head_devices, rows, col_width),
        ],
        [
            own,
            row_sums,
            read,
            base,
            gate_pre,
            gnorm,
            out_gain,
            grad_scan,
            values,
            normed,
            cot_low,
            out_proj,
        ],
        [
            pltpu.VMEM((rows, inner), BF16),
            pltpu.VMEM((blocks, width // blocks, inner), F32),
            pltpu.VMEM((blocks, inner // blocks, width), F32),
        ],
    )

    got_back = lax.optimization_barrier((got_back, early_send))[0]
    (leaving,) = local(back_scan_kernel, [((blocks, share, inner), F32)], [got, got_back])
    grad_end = lax.all_to_all(leaving, "seq", 0, 0).reshape(seqs, nstate, inner)
    near = orders(blocks)[0]
    near_head = orders(head_devices)[0]
    early_chain = Reduce(early_keep, early_send, "seq", near)
    branch_chain = Reduce(branch_keep, branch_send, "head", near_head)
    grad_scan = lax.optimization_barrier((grad_scan, leaving))[0]
    scaled_grad, grad_b, grad_c, gaps = local(
        mix_kernel,
        [
            (full, F32, 0),
            ((seqs, length, nstate), F32, 0),
            ((seqs, length, nstate), F32, 0),
            ((seqs, heads, length), F32, 0),
        ],
        cut(values, states, step_x, exp_cum_x, cum, cum_t, grad_scan, state_in),
        steps=seqs,
    )
    early_chain.step(after=(gaps, grad_end))
    state_keep, state_send = local(
        state_sum_kernel,
        halves(head_devices, rows, part, F32, 1),
        [own, *cut(grad_end, values, step_x, end_x, grad_b, grad_c)],
        steps=seqs,
    )
    state_part = Reduce(state_keep, state_send, "head", near_head).finish()
    value_in, grad_step_t, value_rows, head_rows = local(
        value_kernel,
        [
            ((seqs, PAD + length, inner), F32, 0),
            ((seqs, heads, length), BF16, 0),
            ((taps + 1, inner), F32),
            ((heads, LANES), F32),
        ],
        [
            *cut(grad_end, state_in, values, states, value_slope, value_conv_in),
            conv_value,
            *cut(step_x, exp_cum_x, end_x, step_arg_t),
            decay_log,
            skip_gain,
            *cut(read, grad_scan, scaled_grad, gaps),
        ],
        [pltpu.VMEM((length + 2 * PAD, inner), F32)],
        steps=seqs,
    )
    state_part = hold(state_part, early_chain)
    early_chain.step(after=(value_in,))
    value_lines = width // blocks
    state_lines = part // blocks * (width // inner)
    state_grad_in, state_rows, step_rows, late = local(
        weight_kernel,
        [
            ((seqs, PAD + length, part), F32),
            ((taps + 1, part), F32),
            ((heads, width), F32),
            ((blocks, value_lines + state_lines, inner), BF16),
        ],
        [
            normed,
            value_in,
            grad_step_t,
            state_part,
            own_cols(state_slope, part),
            own_cols(state_conv_in, part),
            own_cols(conv_state, part),
        ],
        [pltpu.VMEM((length + 2 * PAD, part), F32)],
    )
    early_chain.step(after=(late,))
    early_chain = Gather(early_chain.finish(), "seq", near)
    early_chain.step()
    late = lax.all_to_all(late, "seq", 0, 0)
    over = jnp.concatenate([value_in[:, :PAD], state_grad_in[:, :PAD]], axis=2)
    over = shift(over, "seq", -1)
    late = hold(late, early_chain)
    early_chain.step()
    late_values, late_states = local(
        sum_kernel,
        [((blocks, value_lines, inner), BF16), ((state_lines, inner), BF16)],
        [late],
    )
    over = lax.optimization_barrier((over, late_values))[0]
    grad_value_proj = lax.all_to_all(late_values, "seq", 0, 0)
    keep, send, row_part, gain_sum = local(
        back_kernel,
        [
            *halves(head_devices, rows, col_width, BF16, 1),
            ((8, rows), F32, 1),
            ((1, width), F32),
        ],
        [
            own,
            (tokens, 0),
            norm_gain,
            *cut(value_in, state_grad_in, over[:, :, :inner], over[:, :, inner:]),
            value_proj,
            own_cols(state_proj, part),
            (grad_gate, 0),
            gate_proj,
            (grad_step_t, 0),
            step_proj_t,
        ],
        steps=seqs,
    )
    back_chain = Reduce(keep, send, "head", near_head)
    grad_value_proj = grad_value_proj.reshape(width, inner).astype(F32)
    grad_gate_proj, grad_out_proj = local(
        place_kernel,
        [
            ((blocks, value_lines, inner), F32),
            ((blocks, inner // blocks, width), F32),
        ],
        [own, *early_chain.finish()],
    )
    grad_gate_proj = grad_gate_proj.reshape(width, inner)
    grad_out_proj = grad_out_proj.reshape(inner, width)
    state_chain = Gather(late_states, "head", near_head)
    state_chain = Gather(jnp.concatenate(state_chain.finish(), axis=0), "seq", near)
    (grad_state_proj,) = local(
        place_state_kernel,
        [((width, 2 * nstate), F32)],
        [own, *state_chain.finish()],
        [pltpu.VMEM((blocks * head_devices, part // blocks, width), F32)],
    )
    branch = branch_chain.finish().astype(F32)
    own_source = own_cols(tokens.reshape(rows, width), col_width).astype(F32)
    mixed_rows = (own_source + branch).reshape(seqs, length, col_width)
    own_part = back_chain.finish().astype(F32)
    row_mean = sum_all(row_part, "head")[0][:, None] / width
    source = tokens.reshape(rows, width).astype(F32)
    own_scale = lax.rsqrt(jnp.mean(source * source, axis=-1, keepdims=True) + EPS)
    own_unit = own_source * own_scale
    grad_tokens = cot_rows + own_scale * (own_part - own_unit * row_mean)
    grad_tokens = grad_tokens.reshape(seqs, length, col_width)

    def padded(x, lines, lanes):
        return jnp.pad(x, ((0, lines - x.shape[0]), (0, lanes - x.shape[1])))

    state_rows = lax.dynamic_update_slice(
        jnp.zeros((taps + 1, 2 * nstate), F32), state_rows, (0, head_index * part)
    )
    lines = max(heads, taps + 1)
    lanes = max(width, channels + LANES)
    small = jnp.concatenate(
        [
            padded(step_rows, heads, lanes),
            padded(
                jnp.concatenate(
                    [
                        padded(value_rows, lines, inner),
                        padded(state_rows, lines, 2 * nstate),
                        padded(head_rows, lines, LANES),
                    ],
                    axis=1,
                ),
                lines,
                lanes,
            ),
            padded(inner_row, 1, lanes),
            padded(gain_sum, 1, lanes),
        ],
        axis=0,
    )
    small = sum_all(small, "seq")
    whole = sum_all(small[heads:], "head")
    conv_lines = small[heads : heads + lines]
    grad_heads = conv_lines[:heads, channels : channels + 2]
    grad_inner = small[heads + lines, : 2 * inner]
    return (
        mixed_rows,
        grad_tokens,
        whole[lines + 1, :width],
        grad_gate_proj,
        grad_value_proj,
        grad_state_proj,
        jnp.transpose(small[:heads, :width]),
        conv_lines[:taps, :inner],
        conv_lines[taps, :inner],
        whole[:taps, inner:channels],
        whole[taps, inner:channels],
        grad_heads[:, 0],
        grad_heads[:, 1],
        jnp.sum(grad_inner[inner:].reshape(heads, head_dim), axis=1),
        grad_inner[:inner],
        grad_out_proj,
    )


def solution(mesh):
    return jax.shard_map(
        on_device,
        mesh=mesh,
        in_specs=(
            P(None, "seq", None),
            P(),
            P(None, "head"),
            P(None, "head"),
            P(),
            P(None, "head"),
            P(None, "head"),
            P("head"),
            P(),
            P(),
            P("head"),
            P("head"),
            P("head"),
            P("head"),
            P("head", None),
            P(None, "seq", "head"),
        ),
        out_specs=(
            P(None, "seq", "head"),
            P(None, "seq", "head"),
            P(),
            P(None, "head"),
            P(None, "head"),
            P(),
            P(None, "head"),
            P(None, "head"),
            P("head"),
            P(),
            P(),
            P("head"),
            P("head"),
            P("head"),
            P("head"),
            P("head", None),
        ),
        check_vma=False,
    )
```

```python
import functools

import jax
import jax.numpy as jnp
from jax import lax
from jax.experimental import pallas as pl
from jax.experimental.pallas import tpu as pltpu
from jax.sharding import PartitionSpec as P

EPS = 1e-05
F32 = jnp.float32
BF16 = jnp.bfloat16
NN = ((1,), (0,))
NT = ((1,), (1,))
TN = ((0,), (0,))
PAD = 16
LANES = 128


def shift(x, axis, by):
    devices = lax.axis_size(axis)
    pairs = [(i, i + by) for i in range(devices) if 0 <= i + by < devices]
    return lax.ppermute(x, axis, pairs)


def swap(x, axis, mask):
    devices = lax.axis_size(axis)
    return lax.ppermute(x, axis, [(i, i ^ mask) for i in range(devices)])


def masks(axis):
    found, mask = [], 1
    while mask < lax.axis_size(axis):
        found.append(mask)
        mask *= 2
    return found


def sum_all(x, axis):
    for mask in masks(axis):
        x = x + swap(x, axis, mask)
    return x


def orders(axis_size):
    near = [1 << t for t in range(axis_size.bit_length() - 1)]
    return near, near[1:2] + near[:1] + near[2:]


def places(order):
    bits = len(order)
    return [
        sum(((p >> (bits - 1 - t)) & 1) * order[t] for t in range(bits))
        for p in range(1 << bits)
    ]


def add_wide(left, right):
    return (left.astype(F32) + right.astype(F32)).astype(left.dtype)


class Reduce:
    def __init__(self, keep, send, axis, order):
        self.keep, self.send, self.axis, self.order = keep, send, axis, list(order)

    def step(self, after=()):
        got = swap(self.send, self.axis, self.order.pop(0))
        got = lax.optimization_barrier((got, after))[0]
        half = self.keep.shape[0] // 2
        if half == 0:
            self.keep, self.send = add_wide(self.keep[0], got[0]), None
        else:
            self.send = add_wide(self.keep[half:], got[half:])
            self.keep = add_wide(self.keep[:half], got[:half])

    def finish(self):
        while self.order:
            self.step()
        return self.keep


def send_direct(keep, send, axis, order):
    half = keep.shape[0]
    pieces = [keep[p] for p in range(half)] + [send[p] for p in range(half)]
    return [
        swap(piece, axis, mask) if mask else piece
        for piece, mask in zip(pieces, places(order))
    ]


class Gather:
    def __init__(self, x, axis, order):
        self.near, self.far, self.axis, self.order = x[None], None, axis, list(order)

    def step(self):
        if self.far is not None:
            self.near = jnp.concatenate([self.near, self.far], axis=0)
        self.far = swap(self.near, self.axis, self.order.pop())

    def finish(self):
        while self.order:
            self.step()
        return self.near, self.far


def hold(x, *chains):
    held = [(c.keep, c.send) if isinstance(c, Reduce) else (c.near, c.far) for c in chains]
    x, held = lax.optimization_barrier((x, held))
    for chain, state in zip(chains, held):
        if isinstance(chain, Reduce):
            chain.keep, chain.send = state
        else:
            chain.near, chain.far = state
    return x


def dot(left, right, dims=NN):
    return lax.dot_general(left, right, (dims, ((), ())), preferred_element_type=F32)


def parts(x, count):
    found = []
    for _ in range(count):
        term = x.astype(BF16)
        found.append(term)
        x = x - term.astype(F32)
    return found


def dot_fine(left, right, dims=NN):
    left_high, left_low = parts(left, 2)
    right_high, right_low = parts(right, 2)
    return (
        dot(left_high, right_high, dims)
        + dot(left_low, right_high, dims)
        + dot(left_high, right_low, dims)
    )


def dot_left(left, right, dims=NN, count=2):
    return sum(dot(term, right, dims) for term in parts(left, count))


def dot_right(left, right, dims=NN, count=2):
    return sum(dot(left, term, dims) for term in parts(right, count))


def silu(x):
    return x * jax.nn.sigmoid(x)


def silu_slope(inputs):
    sigma = jax.nn.sigmoid(inputs)
    return sigma * (1.0 + inputs * (1.0 - sigma))


def softplus(x):
    return jnp.maximum(x, 0.0) + jnp.log1p(jnp.exp(-jnp.abs(x)))


def iota(shape, dim):
    return lax.broadcasted_iota(jnp.int32, shape, dim)


def spread(heads, inner):
    lane, head = iota((heads, inner), 1), iota((heads, inner), 0)
    size = inner // heads
    inside = (lane >= head * size) & (lane < (head + 1) * size)
    return jnp.where(inside, 1.0, 0.0).astype(BF16)


def lane_blocks(heads, inner):
    size = inner // heads
    for start in range(0, inner, LANES):
        stop = min(start + LANES, inner)
        yield start, stop, range(start // size, stop // size)


def head_lanes(start, stop, head, size, length):
    lane = iota((length, stop - start), 1) + start
    return (lane >= head * size) & (lane < (head + 1) * size)


def local(body, outs, args, scratch=(), steps=1, flops=100_000_000):
    def spec(shape, dim, smem=False):
        if smem:
            return pl.BlockSpec(memory_space=pltpu.SMEM)
        block = [size // steps if at == dim else size for at, size in enumerate(shape)]
        return pl.BlockSpec(
            tuple(block),
            lambda step, dim=dim: tuple(step if at == dim else 0 for at in range(len(shape))),
        )

    pairs = [a if isinstance(a, tuple) else (a, None) for a in args]
    trio = [o if len(o) == 3 else (*o, None) for o in outs]
    size = sum(a.size * a.dtype.itemsize for a, _ in pairs)
    return pl.pallas_call(
        body,
        grid=(steps,),
        out_shape=[jax.ShapeDtypeStruct(shape, dtype) for shape, dtype, _ in trio],
        in_specs=[spec(a.shape, dim, a.dtype == jnp.int32) for a, dim in pairs],
        out_specs=[spec(shape, dim) for shape, _, dim in trio],
        scratch_shapes=list(scratch),
        compiler_params=pltpu.CompilerParams(vmem_limit_bytes=60 * 2**20),
        cost_estimate=pl.CostEstimate(
            flops=flops, bytes_accessed=size // 4, transcendentals=0
        ),
    )(*[a for a, _ in pairs])


def accumulate(ref, value):
    first = pl.program_id(0) == 0

    @pl.when(first)
    def _():
        ref[...] = value

    @pl.when(jnp.logical_not(first))
    def _():
        ref[...] += value


def as_row(ref):
    return ref[...].reshape(1, -1)


def as_column(row):
    count = row.shape[1]
    eye = iota((count, count), 0) == iota((count, count), 1)
    return jnp.sum(jnp.where(eye, row, 0.0), axis=1, keepdims=True)


def first_kernel(
    tokens_ref,
    edge_ref,
    gain_ref,
    value_proj_ref,
    state_proj_ref,
    step_proj_ref,
    conv_value_ref,
    conv_value_bias_ref,
    conv_state_ref,
    conv_state_bias_ref,
    step_bias_ref,
    decay_log_ref,
    normed_ref,
    value_in_ref,
    state_in_ref,
    values_ref,
    states_ref,
    value_slope_ref,
    state_slope_ref,
    step_x_ref,
    exp_cum_x_ref,
    end_x_ref,
    weighted_ref,
    cum_ref,
    cum_t_ref,
    step_arg_t_ref,
    ends_ref,
):
    _, length, _ = tokens_ref.shape
    inner = values_ref.shape[2]
    heads = cum_ref.shape[2]
    nstate = states_ref.shape[2] // 2
    blocks, share = ends_ref.shape[0], ends_ref.shape[1] - 8
    spread_mat = spread(heads, inner)
    row, col = iota((length, length), 0), iota((length, length), 1)
    lower = jnp.where(row >= col, 1.0, 0.0).astype(BF16)
    upper = jnp.where(row <= col, 1.0, 0.0).astype(BF16)
    step_bias = as_row(step_bias_ref)
    rate = jnp.exp(as_row(decay_log_ref))
    for source, first, count in ((edge_ref, 0, PAD), (tokens_ref, PAD, length)):
        x = source[0].astype(F32)
        scale = lax.rsqrt(jnp.mean(x * x, axis=-1, keepdims=True) + EPS)
        normed_ref[0, first : first + count] = (x * scale * as_row(gain_ref)).astype(BF16)
    normed = normed_ref[0, PAD:]
    step_arg = dot(normed, step_proj_ref[...], NT) + step_bias
    step_arg_t = dot(step_proj_ref[...], normed, NT) + as_column(step_bias)
    step_arg_t_ref[0] = step_arg_t
    step = softplus(step_arg)
    cum = dot_right(lower, -step * rate, NN, 3)
    cum_ref[0] = cum
    cum_t_ref[0] = dot_left(-softplus(step_arg_t) * as_column(rate), upper, NN, 3)
    step_x = dot_left(step, spread_mat)
    exp_cum_x = dot_left(jnp.exp(cum), spread_mat)
    end_x = dot_left(jnp.exp(cum[length - 1 :] - cum), spread_mat)
    step_x_ref[0] = step_x
    exp_cum_x_ref[0] = exp_cum_x
    end_x_ref[0] = end_x

    def convolve(proj_ref, weight_ref, bias_ref, in_ref, out_ref, slope_ref):
        taps = weight_ref.shape[0]
        in_ref[0] = dot(normed_ref[0], proj_ref[...])
        conv_out = as_row(bias_ref)
        for tap in range(taps):
            first = PAD - taps + 1 + tap
            conv_out = conv_out + weight_ref[tap : tap + 1] * in_ref[0, first : first + length]
        sigma = jax.nn.sigmoid(conv_out)
        slope_ref[0] = sigma * (1.0 + conv_out * (1.0 - sigma))
        out_ref[0] = conv_out * sigma

    convolve(
        state_proj_ref,
        conv_state_ref,
        conv_state_bias_ref,
        state_in_ref,
        states_ref,
        state_slope_ref,
    )
    convolve(
        value_proj_ref,
        conv_value_ref,
        conv_value_bias_ref,
        value_in_ref,
        values_ref,
        value_slope_ref,
    )
    weighted = end_x * step_x * values_ref[0]
    weighted_ref[0] = weighted
    ends = dot_fine(states_ref[0, :, :nstate], weighted, TN)
    for block in range(blocks):
        ends_ref[block, 0:8] = jnp.broadcast_to(exp_cum_x[length - 1 :], (8, inner))
        ends_ref[block, 8:] = ends[block * share : (block + 1) * share]


def scan_kernel(got_ref, entering_ref):
    running = jnp.zeros(entering_ref.shape[1:], F32)
    for block in range(got_ref.shape[0]):
        entering_ref[block] = running
        running = got_ref[block, 0:1] * running + got_ref[block, 8:]


def back_scan_kernel(got_ref, back_ref, leaving_ref):
    running = jnp.zeros(leaving_ref.shape[1:], F32)
    for block in reversed(range(got_ref.shape[0])):
        leaving_ref[block] = running
        running = got_ref[block, 0:1] * running + back_ref[block]


def inside_kernel(
    normed_ref,
    gate_proj_ref,
    values_ref,
    states_ref,
    step_x_ref,
    cum_ref,
    cum_t_ref,
    cot_ref,
    out_proj_ref,
    skip_ref,
    base_ref,
    gnorm_ref,
    gate_pre_ref,
):
    seqs, length, inner = base_ref.shape
    heads = cum_ref.shape[2]
    size = inner // heads
    nstate = states_ref.shape[2] // 2
    skip = dot_left(as_row(skip_ref), spread(heads, inner), NN, 3)
    causal = iota((length, length), 0) >= iota((length, length), 1)
    for seq in range(seqs):
        gate_pre_ref[seq] = dot(normed_ref[seq, PAD:], gate_proj_ref[...])
        products = dot_fine(states_ref[seq, :, nstate:], states_ref[seq, :, :nstate], NT)
        for start, stop, block_heads in lane_blocks(heads, inner):
            values = values_ref[seq, :, start:stop]
            scaled = parts(values * step_x_ref[seq, :, start:stop], 2)
            total = None
            for head in block_heads:
                gap = cum_ref[seq, :, head : head + 1] - cum_t_ref[seq, head : head + 1, :]
                decay = jnp.exp(jnp.where(causal, gap, -1e30))
                high, low = parts(decay * products, 2)
                part = dot(high, scaled[0]) + dot(low, scaled[0]) + dot(high, scaled[1])
                if total is None:
                    total = part
                else:
                    total = jnp.where(head_lanes(start, stop, head, size, length), part, total)
            base_ref[seq, :, start:stop] = total + skip[:, start:stop] * values
        gnorm_ref[seq] = dot(cot_ref[seq * length : (seq + 1) * length], out_proj_ref[...], NT)


def read_kernel(
    state_ref,
    states_ref,
    exp_cum_x_ref,
    base_ref,
    gate_pre_ref,
    gnorm_ref,
    out_gain_ref,
    read_ref,
    sums_ref,
):
    seqs, length, inner = base_ref.shape
    nstate = states_ref.shape[2] // 2
    ones = jnp.ones((8, inner), BF16)
    for seq in range(seqs):
        read = exp_cum_x_ref[seq] * dot_fine(states_ref[seq, :, nstate:], state_ref[seq])
        read_ref[seq] = read
        gated = (base_ref[seq] + read) * silu(gate_pre_ref[seq])
        squares = dot_right(ones, gated * gated, NT)
        backs = dot_right(ones, gnorm_ref[seq] * as_row(out_gain_ref) * gated, NT)
        row = iota((8, length), 0)
        sums_ref[:, seq * length : (seq + 1) * length] = jnp.where(row == 0, squares, backs)


def gate_kernel(
    sums_ref,
    read_ref,
    base_ref,
    gate_pre_ref,
    gnorm_ref,
    out_gain_ref,
    exp_cum_x_ref,
    states_ref,
    grad_scan_ref,
    back_ref,
    *,
    inner_total,
):
    nstate = states_ref.shape[2] // 2
    blocks, share = back_ref.shape[0], back_ref.shape[1]
    sums = jnp.transpose(sums_ref[...])
    scale = lax.rsqrt(sums[:, 0:1] / inner_total + EPS)
    back_mean = scale * sums[:, 1:2] / inner_total
    gate_act = silu(gate_pre_ref[0])
    unit = (base_ref[0] + read_ref[0]) * gate_act * scale
    grad_gated = scale * (gnorm_ref[0] * as_row(out_gain_ref) - unit * back_mean)
    grad_scan = grad_gated * gate_act
    grad_scan_ref[0] = grad_scan
    back = dot_fine(states_ref[0, :, nstate:], exp_cum_x_ref[0] * grad_scan, TN)
    for block in range(blocks):
        back_ref[block] = back[block * share : (block + 1) * share]


def cut_lines(held, value):
    count = held.shape[1]
    for piece in range(held.shape[0]):
        held[piece] = value[piece * count : (piece + 1) * count]


def stacked(lines, lanes):
    return [lines[:, at : at + lanes] for at in range(0, lines.shape[1], lanes)]


def ordered_piece(own, at, value, keep_ref, send_ref):
    half = keep_ref.shape[0]
    for p, mask in enumerate(places(orders(2 * half)[0])):

        @pl.when((own ^ mask) == at)
        def _():
            (keep_ref if p < half else send_ref)[p % half, :, : value.shape[1]] = value


def low_kernel(
    own_ref,
    sums_ref,
    read_ref,
    base_ref,
    gate_pre_ref,
    gnorm_ref,
    out_gain_ref,
    grad_scan_ref,
    values_ref,
    normed_ref,
    cot_ref,
    out_proj_ref,
    proj_ref,
    grad_gate_ref,
    rows_ref,
    gain_row_ref,
    keep_ref,
    send_ref,
    branch_keep_ref,
    branch_send_ref,
    gate_low,
    grad_gate_proj,
    grad_out_proj,
    *,
    inner_total,
):
    seqs, length, inner = base_ref.shape
    gain_sum = jnp.zeros((1, inner), F32)
    skip_sum = jnp.zeros((1, inner), F32)
    pieces = 2 * branch_keep_ref.shape[0]
    col_width = branch_keep_ref.shape[2]
    total = None
    for seq in range(seqs):
        sums = jnp.transpose(sums_ref[:, seq * length : (seq + 1) * length])
        scale = lax.rsqrt(sums[:, 0:1] / inner_total + EPS)
        back_mean = scale * sums[:, 1:2] / inner_total
        gate_pre = gate_pre_ref[seq]
        sigma = jax.nn.sigmoid(gate_pre)
        scan_out = base_ref[seq] + read_ref[seq]
        unit = scan_out * gate_pre * sigma * scale
        gnorm = gnorm_ref[seq]
        gate_low[seq * length : (seq + 1) * length] = (unit * as_row(out_gain_ref)).astype(BF16)
        grad_gated = scale * (gnorm * as_row(out_gain_ref) - unit * back_mean)
        slope = sigma * (1.0 + gate_pre * (1.0 - sigma))
        grad_gate = (grad_gated * scan_out * slope).astype(BF16)
        grad_gate_ref[seq] = grad_gate
        part = dot(normed_ref[seq, PAD:], grad_gate, TN)
        total = part if total is None else total + part
        gain_sum = gain_sum + jnp.sum(gnorm * unit, axis=0, keepdims=True)
        skip_sum = skip_sum + jnp.sum(
            grad_scan_ref[seq] * values_ref[seq], axis=0, keepdims=True
        )
    rows_ref[:, :inner] = gain_sum
    rows_ref[:, inner:] = skip_sum
    ones = jnp.ones((8, inner), BF16)
    gain_row_ref[...] = dot_right(ones, total * proj_ref[...].astype(F32), NT)
    cut_lines(grad_gate_proj, total)
    cut_lines(grad_out_proj, dot(gate_low[...], cot_ref[...], TN))
    blocks = 2 * keep_ref.shape[0]
    for p, mask in enumerate(places(orders(blocks)[0])):
        at = own_ref[0] ^ mask
        ref = keep_ref if p < blocks // 2 else send_ref
        value = jnp.concatenate(
            [grad_gate_proj[at], *stacked(grad_out_proj[at], inner)], axis=0
        )
        ref[p % (blocks // 2)] = value.astype(BF16)
    branch = dot(gate_low[...], out_proj_ref[...])
    for piece in range(pieces):
        value = branch[:, piece * col_width : (piece + 1) * col_width].astype(BF16)
        ordered_piece(own_ref[1], piece, value, branch_keep_ref, branch_send_ref)


def mix_kernel(
    values_ref,
    states_ref,
    step_x_ref,
    exp_cum_x_ref,
    cum_ref,
    cum_t_ref,
    grad_scan_ref,
    state_ref,
    scaled_grad_ref,
    grad_b_ref,
    grad_c_ref,
    gaps_ref,
):
    seqs, length, inner = grad_scan_ref.shape
    heads = cum_ref.shape[2]
    size = inner // heads
    nstate = states_ref.shape[2] // 2
    causal = iota((length, length), 0) >= iota((length, length), 1)
    ones = jnp.ones((8, length), BF16)
    for seq in range(seqs):
        b_rows = states_ref[seq, :, :nstate]
        c_rows = states_ref[seq, :, nstate:]
        products = dot_fine(c_rows, b_rows, NT)
        grad_products = jnp.zeros((length, length), F32)
        for start, stop, block_heads in lane_blocks(heads, inner):
            scaled = values_ref[seq, :, start:stop] * step_x_ref[seq, :, start:stop]
            scaled_high, scaled_low = parts(scaled, 2)
            scan_high, scan_low = parts(grad_scan_ref[seq, :, start:stop], 2)
            total = None
            for head in block_heads:
                gap = cum_ref[seq, :, head : head + 1] - cum_t_ref[seq, head : head + 1, :]
                decay = jnp.exp(jnp.where(causal, gap, -1e30))
                own = head_lanes(start, stop, head, size, length)
                own_high = jnp.where(own, scan_high, jnp.zeros_like(scan_high))
                own_low = jnp.where(own, scan_low, jnp.zeros_like(scan_low))
                grad_mix = (
                    dot(own_high, scaled_high, NT)
                    + dot(own_low, scaled_high, NT)
                    + dot(own_high, scaled_low, NT)
                )
                grad_decayed = grad_mix * decay
                grad_products = grad_products + grad_decayed
                related = (grad_decayed * products).astype(BF16)
                gaps = dot(ones, related, NT) - dot(ones, related)
                gaps_ref[seq, head : head + 1] = gaps[0:1]
                part = dot((decay * products).astype(BF16), own_high, TN)
                total = part if total is None else total + part
            scaled_grad_ref[seq, :, start:stop] = total
        carried = exp_cum_x_ref[seq] * grad_scan_ref[seq]
        grad_c_ref[seq] = dot_fine(grad_products, b_rows) + dot_fine(
            carried, state_ref[seq], NT
        )
        grad_b_ref[seq] = dot_fine(grad_products, c_rows, TN)


def state_sum_kernel(
    own_ref,
    grad_end_ref,
    weighted_ref,
    grad_b_ref,
    grad_c_ref,
    keep_ref,
    send_ref,
):
    pieces, part = 2 * keep_ref.shape[0], keep_ref.shape[2]
    grad_b = grad_b_ref[0] + dot_fine(weighted_ref[0], grad_end_ref[0], NT)
    both = jnp.concatenate([grad_b, grad_c_ref[0]], axis=1)
    for piece in range(pieces):
        value = both[:, piece * part : (piece + 1) * part]
        ordered_piece(own_ref[1], piece, value, keep_ref, send_ref)


def conv_back(grad_out, in_ref, weight_ref, seq, around):
    length = grad_out.shape[0]
    taps = weight_ref.shape[0]
    around[PAD : PAD + length] = grad_out
    grad_in = None
    sums = []
    for tap in range(taps):
        first = PAD - taps + 1 + tap
        sums.append(
            jnp.sum(grad_out * in_ref[seq, first : first + length], axis=0, keepdims=True)
        )
        first = taps - 1 - tap
        part = weight_ref[tap : tap + 1] * around[first : first + PAD + length]
        grad_in = part if grad_in is None else grad_in + part
    sums.append(jnp.sum(grad_out, axis=0, keepdims=True))
    return grad_in, jnp.concatenate(sums, axis=0)


def clear_edges(around):
    zeros = jnp.zeros((PAD, around.shape[1]), F32)
    around[0:PAD] = zeros
    around[around.shape[0] - PAD :] = zeros


def value_kernel(
    grad_end_ref,
    state_ref,
    values_ref,
    states_ref,
    slope_ref,
    conv_in_ref,
    conv_weight_ref,
    step_x_ref,
    exp_cum_x_ref,
    end_x_ref,
    step_arg_t_ref,
    decay_log_ref,
    skip_ref,
    read_ref,
    grad_scan_ref,
    scaled_grad_ref,
    gaps_ref,
    grad_in_ref,
    grad_step_t_ref,
    conv_rows_ref,
    head_rows_ref,
    around,
):
    _, length, inner = values_ref.shape
    heads = gaps_ref.shape[1]
    nstate = states_ref.shape[2] // 2
    spread_mat = spread(heads, inner)
    row, col = iota((length, length), 0), iota((length, length), 1)
    lower = jnp.where(row >= col, 1.0, 0.0).astype(BF16)
    rate_t = as_column(jnp.exp(as_row(decay_log_ref)))
    skip = dot_left(as_row(skip_ref), spread_mat, NN, 3)
    last = iota((heads, length), 1) == length - 1
    clear_edges(around)
    values = values_ref[0]
    grad_end = grad_end_ref[0]
    step_x = step_x_ref[0]
    grad_scan = grad_scan_ref[0]
    end_proj = end_x_ref[0] * dot(
        states_ref[0, :, :nstate].astype(BF16), grad_end.astype(BF16)
    )
    scaled_grad = scaled_grad_ref[0] + end_proj
    grad_in, conv_rows = conv_back(
        (skip * grad_scan + step_x * scaled_grad) * slope_ref[0],
        conv_in_ref,
        conv_weight_ref,
        0,
        around,
    )
    grad_in_ref[0] = grad_in
    end_terms = dot_right(spread_mat, step_x * values * end_proj, NT)
    crossed = jnp.sum(grad_end * state_ref[0], axis=0, keepdims=True)
    crossed = crossed * exp_cum_x_ref[0, length - 1 :]
    last_term = jnp.sum(end_terms, axis=1, keepdims=True) + jnp.sum(
        jnp.where(spread_mat.astype(F32) > 0.0, crossed, 0.0), axis=1, keepdims=True
    )
    grad_cum = (
        gaps_ref[0] + dot_right(spread_mat, grad_scan * read_ref[0], NT) - end_terms
    ) + jnp.where(last, last_term, 0.0)
    grad_log = dot_left(grad_cum, lower, NN, 3)
    step_arg = step_arg_t_ref[0]
    rate_sum = -jnp.sum(grad_log * softplus(step_arg), axis=1, keepdims=True)
    grad_step = dot_right(spread_mat, values * scaled_grad, NT) - grad_log * rate_t
    grad_step = grad_step * jax.nn.sigmoid(step_arg)
    bias_sum = jnp.sum(grad_step, axis=1, keepdims=True)
    grad_step_t_ref[0] = grad_step.astype(BF16)
    lane = iota((heads, LANES), 1)
    accumulate(conv_rows_ref, conv_rows)
    accumulate(head_rows_ref, jnp.where(lane == 0, bias_sum, rate_sum * rate_t))


def small_places(heads, taps, lanes):
    return lanes - LANES, heads + max(heads, taps)


def weight_kernel(
    own_ref,
    normed_ref,
    value_in_ref,
    grad_step_t_ref,
    state_grad_ref,
    slope_ref,
    conv_in_ref,
    conv_weight_ref,
    gain_ref,
    gate_gain_row_ref,
    value_proj_ref,
    state_proj_t_ref,
    step_proj_t_ref,
    value_rows_ref,
    head_rows_ref,
    inner_row_ref,
    state_in_ref,
    late_ref,
    around,
    small,
    slope,
    conv_in,
    conv_weight,
    *,
    pieces,
):
    seqs, length, part = slope.shape
    for piece in range(pieces):

        @pl.when(own_ref[1] == piece)
        def _():
            lanes = slice(piece * part, (piece + 1) * part)
            slope[...] = slope_ref[:, :, lanes]
            conv_in[...] = conv_in_ref[:, :, lanes]
            conv_weight[...] = conv_weight_ref[:, lanes]

    width = normed_ref.shape[2]
    blocks, _, inner = late_ref.shape
    value_total = state_total = step_total = conv_total = None

    def add(total, part):
        return part if total is None else total + part

    clear_edges(around)
    for seq in range(seqs):
        normed = normed_ref[seq]
        grad = state_grad_ref[seq * length : (seq + 1) * length] * slope[seq]
        grad_in, conv_rows = conv_back(grad, conv_in, conv_weight, seq, around)
        state_in_ref[seq] = grad_in
        conv_total = add(conv_total, conv_rows)
        value_total = add(value_total, dot(normed, value_in_ref[seq].astype(BF16), TN))
        state_total = add(state_total, dot(grad_in.astype(BF16), normed, TN))
        step_total = add(step_total, dot(grad_step_t_ref[seq], normed_ref[seq, PAD:]))
    ones = jnp.ones((8, inner), BF16)
    gain_row = gate_gain_row_ref[...] + dot_right(
        ones, value_total * value_proj_ref[...].astype(F32), NT
    )
    gain_row = (
        gain_row[0:1]
        + jnp.sum(state_total * state_proj_t_ref[...].astype(F32), axis=0, keepdims=True)
        + jnp.sum(step_total * step_proj_t_ref[...].astype(F32), axis=0, keepdims=True)
    )
    heads, taps = step_total.shape[0], value_rows_ref.shape[0]
    heads_at, last = small_places(heads, taps, small.shape[1])
    small[...] = jnp.zeros(small.shape, F32)
    small[:heads, :width] = step_total
    small[heads : heads + taps, :inner] = value_rows_ref[...]
    for piece in range(pieces):

        @pl.when(own_ref[1] == piece)
        def _():
            first = inner + piece * part
            small[heads : heads + taps, first : first + part] = conv_total

    small[heads : 2 * heads, heads_at:] = head_rows_ref[...]
    small[last : last + 1, : 2 * inner] = inner_row_ref[...]
    small[last + 1 : last + 2, :width] = gain_row / as_row(gain_ref)
    small_rows = jnp.concatenate(stacked(small[...], inner), axis=0)
    small_lines = small_rows.shape[0] // blocks
    value_lines = width // blocks
    state_lines = state_total.shape[0] // blocks
    for block in range(blocks):
        value = value_total[block * value_lines : (block + 1) * value_lines]
        state = state_total[block * state_lines : (block + 1) * state_lines]
        lines = small_rows[block * small_lines : (block + 1) * small_lines]
        value = [value, *stacked(state, inner), *[x.astype(F32) for x in parts(lines, 2)]]
        spare = late_ref.shape[1] - sum(x.shape[0] for x in value)
        if spare:
            value.append(jnp.zeros((spare, inner), F32))
        late_ref[block] = jnp.concatenate(value, axis=0).astype(BF16)


def sum_kernel(got_ref, out_ref, *, first, lines):
    total = got_ref[0].astype(F32)
    for block in range(1, got_ref.shape[0]):
        total = total + got_ref[block].astype(F32)
    small = total[first : first + lines] + total[first + lines : first + 2 * lines]
    small = [x.astype(F32) for x in parts(small, 2)]
    spare = [total[first + 2 * lines :]] if total.shape[0] > first + 2 * lines else []
    total = jnp.concatenate([total[:first], *small, *spare], axis=0).astype(BF16)
    for block in range(out_ref.shape[0]):
        out_ref[block] = total


def place_kernel(own_ref, near_ref, far_ref, gate_ref, out_ref):
    blocks, lines, inner = gate_ref.shape
    count = out_ref.shape[1]
    for p, mask in enumerate(places(orders(blocks)[0])):
        ref = near_ref if p < blocks // 2 else far_ref
        value = ref[p % (blocks // 2)].astype(F32)
        at = own_ref[0] ^ mask
        gate_ref[at] = value[:lines]
        for group in range(out_ref.shape[2] // inner):
            first = lines + group * count
            out_ref[at, :, group * inner : (group + 1) * inner] = value[first : first + count]


def back_kernel(
    own_ref,
    tokens_ref,
    gain_ref,
    value_in_ref,
    state_in_ref,
    value_over_ref,
    state_over_ref,
    value_proj_ref,
    state_proj_t_ref,
    grad_gate_ref,
    gate_proj_ref,
    grad_step_t_ref,
    step_proj_t_ref,
    keep_ref,
    send_ref,
    *,
    col_width,
):
    _, length, width = tokens_ref.shape
    pieces = 2 * keep_ref.shape[0]
    def whole(in_ref, over_ref, seq):
        return jnp.concatenate(
            [
                in_ref[seq, PAD:length].astype(BF16),
                (in_ref[seq, length:] + over_ref[seq]).astype(BF16),
            ],
            axis=0,
        )

    x = tokens_ref[0].astype(F32)
    unit = x * lax.rsqrt(jnp.mean(x * x, axis=-1, keepdims=True) + EPS)
    normed_grad = (
        dot(whole(value_in_ref, value_over_ref, 0), value_proj_ref[...], NT)
        + dot(whole(state_in_ref, state_over_ref, 0), state_proj_t_ref[...])
        + dot(grad_gate_ref[0], gate_proj_ref[...], NT)
        + dot(grad_step_t_ref[0], step_proj_t_ref[...], TN)
    )
    unit_grad = normed_grad * as_row(gain_ref)
    row_sum = jnp.sum(unit_grad * unit, axis=-1, keepdims=True).astype(BF16)
    row_sum = jnp.broadcast_to(row_sum, (length, LANES))
    for half_ref in (keep_ref, send_ref):
        for p in range(pieces // 2):
            half_ref[p, :, half_ref.shape[2] - LANES :] = row_sum
    for piece in range(pieces):
        value = unit_grad[:, piece * col_width : (piece + 1) * col_width].astype(BF16)
        ordered_piece(own_ref[1], piece, value, keep_ref, send_ref)


def last_kernel(
    own_ref,
    near_ref,
    far_ref,
    state_proj_ref,
    norm_gain_ref,
    step_proj_ref,
    conv_value_ref,
    conv_value_bias_ref,
    conv_state_ref,
    conv_state_bias_ref,
    step_bias_ref,
    decay_log_ref,
    skip_gain_ref,
    out_gain_ref,
    held,
    smalls,
):
    half, blocks, _, inner = near_ref.shape
    pieces, _, each, width = held.shape
    _, lines, lanes = smalls.shape
    state_lines = each * width // inner
    small_lines = lines * lanes // inner // blocks
    for p, mask in enumerate(places(orders(2 * half)[0])):
        ref = near_ref if p < half else far_ref
        at = own_ref[1] ^ mask
        small = []
        for block in range(blocks):
            value = ref[p % half, block].astype(F32)
            for group in range(width // inner):
                held[at, block, :, group * inner : (group + 1) * inner] = value[
                    group * each : (group + 1) * each
                ]
            high = value[state_lines : state_lines + small_lines]
            small.append(high + value[state_lines + small_lines : state_lines + 2 * small_lines])
        small = jnp.concatenate(small, axis=0)
        smalls[at] = jnp.concatenate(
            [small[first : first + lines] for first in range(0, small.shape[0], lines)], axis=1
        )
    state_proj_ref[...] = jnp.transpose(held[...].reshape(-1, width))
    whole = smalls[0]
    for piece in range(1, pieces):
        whole = whole + smalls[piece]
    small = smalls[own_ref[1]]
    heads = step_proj_ref.shape[0]
    taps = conv_value_ref.shape[0]
    channels = inner + conv_state_ref.shape[1]
    heads_at, last = small_places(heads, taps + 1, lanes)
    norm_gain_ref[...] = whole[last + 1, :width]
    step_proj_ref[...] = small[:heads, :width]
    conv_value_ref[...] = small[heads : heads + taps, :inner]
    conv_value_bias_ref[...] = small[heads + taps, :inner]
    conv_state_ref[...] = whole[heads : heads + taps, inner:channels]
    conv_state_bias_ref[...] = whole[heads + taps, inner:channels]
    sums = small[heads : 2 * heads, heads_at : heads_at + 2]
    eye = iota((heads, heads), 0) == iota((heads, heads), 1)
    step_bias_ref[...] = jnp.sum(jnp.where(eye, sums[:, 0:1], 0.0), axis=0)
    decay_log_ref[...] = jnp.sum(jnp.where(eye, sums[:, 1:2], 0.0), axis=0)
    row = small[last : last + 1, : 2 * inner]
    out_gain_ref[...] = row[0, :inner]
    skip = dot_left(row[:, inner:], spread(heads, inner), NT, 3)
    skip_gain_ref[...] = skip.reshape(heads)


def on_device(
    tokens,
    norm_gain,
    gate_proj,
    value_proj,
    state_proj,
    step_proj,
    conv_value,
    conv_value_bias,
    conv_state,
    conv_state_bias,
    step_bias,
    decay_log,
    skip_gain,
    out_gain,
    out_proj,
    cotangent,
):
    seqs, length, width = tokens.shape
    rows = seqs * length
    heads = step_proj.shape[1]
    inner = gate_proj.shape[1]
    head_dim = inner // heads
    nstate = state_proj.shape[1] // 2
    taps = conv_value.shape[0]
    channels = inner + 2 * nstate
    head_devices = lax.axis_size("head")
    blocks = lax.axis_size("seq")
    head_index = lax.axis_index("head")
    own = jnp.stack([lax.axis_index("seq"), head_index]).astype(jnp.int32)
    col_width = width // head_devices
    share = seqs * nstate // blocks
    part = 2 * nstate // head_devices
    full = (seqs, length, inner)
    inner_total = inner * head_devices

    def own_cols(x, size):
        return lax.dynamic_slice_in_dim(x, head_index * size, size, x.ndim - 1)

    def cut(*arrays):
        return [(x, 0) for x in arrays]

    edge_tokens = shift(tokens[:, length - PAD :, :], "seq", 1)
    step_proj_t = jnp.transpose(step_proj)
    state_proj_t = jnp.transpose(state_proj)
    state_proj_t = lax.dynamic_slice_in_dim(state_proj_t, head_index * part, part, 0)
    (
        normed,
        value_conv_in,
        state_conv_in,
        values,
        states,
        value_slope,
        state_slope,
        step_x,
        exp_cum_x,
        end_x,
        weighted,
        cum,
        cum_t,
        step_arg_t,
        ends,
    ) = local(
        first_kernel,
        [
            ((seqs, PAD + length, width), BF16, 0),
            ((seqs, PAD + length, inner), F32, 0),
            ((seqs, PAD + length, 2 * nstate), F32, 0),
            (full, F32, 0),
            ((seqs, length, 2 * nstate), F32, 0),
            (full, F32, 0),
            ((seqs, length, 2 * nstate), F32, 0),
            (full, F32, 0),
            (full, F32, 0),
            (full, F32, 0),
            (full, F32, 0),
            ((seqs, length, heads), F32, 0),
            ((seqs, heads, length), F32, 0),
            ((seqs, heads, length), F32, 0),
            ((blocks, 8 + share, inner), F32, 0),
        ],
        [
            *cut(tokens, edge_tokens),
            norm_gain,
            value_proj,
            state_proj,
            step_proj_t,
            conv_value,
            conv_value_bias,
            conv_state,
            conv_state_bias,
            step_bias,
            decay_log,
        ],
        steps=seqs,
    )
    got = lax.all_to_all(ends, "seq", 0, 0)
    cot_rows = cotangent.reshape(rows, col_width)
    cot_low, _ = lax.optimization_barrier((cot_rows.astype(BF16), ends))
    cot_low = lax.all_gather(cot_low, "head", axis=1, tiled=True)
    got, cot_low = lax.optimization_barrier((got, cot_low))
    (entering,) = local(scan_kernel, [((blocks, share, inner), F32)], [got])
    state_in = lax.all_to_all(entering, "seq", 0, 0).reshape(seqs, nstate, inner)
    base, gnorm, gate_pre = local(
        inside_kernel,
        [(full, F32, 0), (full, F32, 0), (full, F32, 0)],
        [
            (normed, 0),
            gate_proj,
            *cut(values, states, step_x, cum, cum_t, cot_low),
            out_proj,
            skip_gain,
        ],
        steps=seqs,
    )
    read, row_sums = local(
        read_kernel,
        [(full, F32, 0), ((8, rows), F32, 1)],
        [*cut(state_in, states, exp_cum_x, base, gate_pre, gnorm), out_gain],
        steps=seqs,
    )
    row_sums = sum_all(row_sums, "head")
    grad_scan, back = local(
        functools.partial(gate_kernel, inner_total=inner_total),
        [(full, F32, 0), ((blocks, share, inner), F32, 0)],
        [
            (row_sums, 1),
            *cut(read, base, gate_pre, gnorm),
            out_gain,
            *cut(exp_cum_x, states),
        ],
        steps=seqs,
    )
    got_back = lax.all_to_all(back, "seq", 0, 0)

    def halves(axis_size, lines, lanes, dtype=BF16, dim=None):
        return [((axis_size // 2, lines, lanes), dtype, dim)] * 2

    (
        grad_gate,
        inner_row,
        gate_gain_row,
        early_keep,
        early_send,
        branch_keep,
        branch_send,
    ) = local(
        functools.partial(low_kernel, inner_total=inner_total),
        [
            (full, BF16),
            ((1, 2 * inner), F32),
            ((8, width), F32),
            *halves(blocks, 2 * (width // blocks), inner),
            *halves(head_devices, rows, col_width),
        ],
        [
            own,
            row_sums,
            read,
            base,
            gate_pre,
            gnorm,
            out_gain,
            grad_scan,
            values,
            normed,
            cot_low,
            out_proj,
            gate_proj,
        ],
        [
            pltpu.VMEM((rows, inner), BF16),
            pltpu.VMEM((blocks, width // blocks, inner), F32),
            pltpu.VMEM((blocks, inner // blocks, width), F32),
        ],
    )

    got_back = lax.optimization_barrier((got_back, early_send))[0]
    (leaving,) = local(back_scan_kernel, [((blocks, share, inner), F32)], [got, got_back])
    grad_end = lax.all_to_all(leaving, "seq", 0, 0).reshape(seqs, nstate, inner)
    near = orders(blocks)[0]
    near_head = orders(head_devices)[0]
    even = places(near)[: blocks // 2]
    branch_chain = Reduce(branch_keep, branch_send, "head", near_head)
    grad_scan = lax.optimization_barrier((grad_scan, leaving))[0]
    scaled_grad, grad_b, grad_c, gaps = local(
        mix_kernel,
        [
            (full, F32, 0),
            ((seqs, length, nstate), F32, 0),
            ((seqs, length, nstate), F32, 0),
            ((seqs, heads, length), F32, 0),
        ],
        cut(values, states, step_x, exp_cum_x, cum, cum_t, grad_scan, state_in),
        steps=seqs,
    )
    early = lax.optimization_barrier((swap(early_send, "seq", 1), gaps))[0]
    early = add_wide(early_keep, early)
    grad_end, early = lax.optimization_barrier((grad_end, early))
    early = [
        swap(early[p], "seq", mask) if mask else early[p] for p, mask in enumerate(even)
    ]
    state_keep, state_send = local(
        state_sum_kernel,
        halves(head_devices, rows, part, F32, 1),
        [own, *cut(grad_end, weighted, grad_b, grad_c)],
        steps=seqs,
    )
    state_part = send_direct(state_keep, state_send, "head", near_head)
    state_part = sum(state_part[1:], state_part[0])
    value_in, grad_step_t, value_rows, head_rows = local(
        value_kernel,
        [
            ((seqs, PAD + length, inner), F32, 0),
            ((seqs, heads, length), BF16, 0),
            ((taps + 1, inner), F32),
            ((heads, LANES), F32),
        ],
        [
            *cut(grad_end, state_in, values, states, value_slope, value_conv_in),
            conv_value,
            *cut(step_x, exp_cum_x, end_x, step_arg_t),
            decay_log,
            skip_gain,
            *cut(read, grad_scan, scaled_grad, gaps),
        ],
        [pltpu.VMEM((length + 2 * PAD, inner), F32)],
        steps=seqs,
    )
    value_lines = width // blocks
    state_lines = part // blocks * (width // inner)
    small_lanes = max(width, channels + LANES)
    small_rows = -(-(heads + max(heads, taps + 1) + 2) // 8) * 8
    small_lines = small_rows * (small_lanes // inner) // blocks
    late_lines = -(-(value_lines + state_lines + 2 * small_lines) // 16) * 16
    state_grad_in, late = local(
        functools.partial(weight_kernel, pieces=head_devices),
        [
            ((seqs, PAD + length, part), F32),
            ((blocks, late_lines, inner), BF16),
        ],
        [
            own,
            normed,
            value_in,
            grad_step_t,
            state_part,
            state_slope,
            state_conv_in,
            conv_state,
            norm_gain,
            gate_gain_row,
            value_proj,
            state_proj_t,
            step_proj_t,
            value_rows,
            head_rows,
            inner_row,
        ],
        [
            pltpu.VMEM((length + 2 * PAD, part), F32),
            pltpu.VMEM((small_rows, small_lanes), F32),
            pltpu.VMEM((seqs, length, part), F32),
            pltpu.VMEM((seqs, PAD + length, part), F32),
            pltpu.VMEM((taps, part), F32),
        ],
    )
    late, early = lax.optimization_barrier((late, early))
    early = sum(x.astype(F32) for x in early).astype(BF16)
    early = [swap(early, "seq", mask) if mask else early for mask in even]
    late = lax.all_to_all(late, "seq", 0, 0)
    over = jnp.concatenate([value_in[:, :PAD], state_grad_in[:, :PAD]], axis=2)
    over = shift(over, "seq", -1)
    branch = branch_chain.finish().astype(F32)
    own_source = own_cols(tokens.reshape(rows, width), col_width).astype(F32)
    mixed_rows = jnp.swapaxes((own_source + branch).reshape(seqs, length, col_width), 1, 2)
    back_width = -(-(col_width + 1) // LANES) * LANES
    keep, send = local(
        functools.partial(back_kernel, col_width=col_width),
        [
            *halves(head_devices, rows, back_width, BF16, 1),
        ],
        [
            own,
            (tokens, 0),
            norm_gain,
            *cut(value_in, state_grad_in, over[:, :, :inner], over[:, :, inner:]),
            value_proj,
            state_proj_t,
            (grad_gate, 0),
            gate_proj,
            (grad_step_t, 0),
            step_proj_t,
        ],
        steps=seqs,
    )
    early = jnp.stack(early)
    late, mixed_rows, early, keep, send = lax.optimization_barrier(
        (late, mixed_rows, early, keep, send)
    )
    early_far = swap(early, "seq", 1)
    (late_values,) = local(
        functools.partial(
            sum_kernel, first=value_lines + state_lines, lines=small_lines
        ),
        [((blocks, late_lines, inner), BF16)],
        [late],
    )
    late = lax.all_to_all(late_values, "seq", 0, 0)
    own_part = send_direct(keep, send, "head", near_head)
    own_part = sum(x.astype(F32) for x in own_part)
    row_mean = own_part[:, back_width - 1 :] / width
    own_part = own_part[:, :col_width]
    source = tokens.reshape(rows, width).astype(F32)
    own_scale = lax.rsqrt(jnp.mean(source * source, axis=-1, keepdims=True) + EPS)
    own_unit = own_source * own_scale
    grad_tokens = cot_rows + own_scale * (own_part - own_unit * row_mean)
    grad_tokens = jnp.swapaxes(grad_tokens.reshape(seqs, length, col_width), 1, 2)
    late, grad_tokens = lax.optimization_barrier((late, grad_tokens))
    grad_value_proj = late[:, :value_lines].reshape(width, inner).astype(F32)
    grad_gate_proj, grad_out_proj = local(
        place_kernel,
        [
            ((blocks, value_lines, inner), F32),
            ((blocks, inner // blocks, width), F32),
        ],
        [own, early, early_far],
    )
    grad_gate_proj = grad_gate_proj.reshape(width, inner)
    grad_out_proj = grad_out_proj.reshape(inner, width)
    state_chain = Gather(late[:, value_lines:], "head", near_head)
    state_chain.step()
    done = (grad_gate_proj, grad_out_proj, mixed_rows, grad_tokens)
    grad_gate_proj, grad_out_proj, mixed_rows, grad_tokens = hold(done, state_chain)
    (
        grad_state_proj,
        grad_norm_gain,
        grad_step_proj,
        grad_conv_value,
        grad_conv_value_bias,
        grad_conv_state,
        grad_conv_state_bias,
        grad_step_bias,
        grad_decay_log,
        grad_skip_gain,
        grad_out_gain,
    ) = local(
        last_kernel,
        [
            ((width, 2 * nstate), F32),
            ((width,), F32),
            ((heads, width), F32),
            ((taps, inner), F32),
            ((inner,), F32),
            ((taps, 2 * nstate), F32),
            ((2 * nstate,), F32),
            ((heads,), F32),
            ((heads,), F32),
            ((heads,), F32),
            ((inner,), F32),
        ],
        [own, *state_chain.finish()],
        [
            pltpu.VMEM((head_devices, blocks, part // blocks, width), F32),
            pltpu.VMEM((head_devices, small_rows, small_lanes), F32),
        ],
    )
    return (
        jnp.swapaxes(mixed_rows, 1, 2),
        jnp.swapaxes(grad_tokens, 1, 2),
        grad_norm_gain,
        grad_gate_proj,
        grad_value_proj,
        grad_state_proj,
        jnp.transpose(grad_step_proj),
        grad_conv_value,
        grad_conv_value_bias,
        grad_conv_state,
        grad_conv_state_bias,
        grad_step_bias,
        grad_decay_log,
        grad_skip_gain,
        grad_out_gain,
        grad_out_proj,
    )


def solution(mesh):
    return jax.shard_map(
        on_device,
        mesh=mesh,
        in_specs=(
            P(None, "seq", None),
            P(),
            P(None, "head"),
            P(None, "head"),
            P(),
            P(None, "head"),
            P(None, "head"),
            P("head"),
            P(),
            P(),
            P("head"),
            P("head"),
            P("head"),
            P("head"),
            P("head", None),
            P(None, "seq", "head"),
        ),
        out_specs=(
            P(None, "seq", "head"),
            P(None, "seq", "head"),
            P(),
            P(None, "head"),
            P(None, "head"),
            P(),
            P(None, "head"),
            P(None, "head"),
            P("head"),
            P(),
            P(),
            P("head"),
            P("head"),
            P("head"),
            P("head"),
            P("head", None),
        ),
        check_vma=False,
    )
```

```python
import functools

import jax
import jax.numpy as jnp
from jax import lax
from jax.experimental import pallas as pl
from jax.experimental.pallas import tpu as pltpu
from jax.sharding import PartitionSpec as P

EPS = 1e-05
F32 = jnp.float32
BF16 = jnp.bfloat16
NN = ((1,), (0,))
NT = ((1,), (1,))
TN = ((0,), (0,))
PAD = 16
LANES = 128


def shift(x, axis, by):
    devices = lax.axis_size(axis)
    pairs = [(i, i + by) for i in range(devices) if 0 <= i + by < devices]
    return lax.ppermute(x, axis, pairs)


def swap(x, axis, mask):
    devices = lax.axis_size(axis)
    return lax.ppermute(x, axis, [(i, i ^ mask) for i in range(devices)])


def masks(axis):
    found, mask = [], 1
    while mask < lax.axis_size(axis):
        found.append(mask)
        mask *= 2
    return found


def sum_all(x, axis):
    for mask in masks(axis):
        x = x + swap(x, axis, mask)
    return x


def orders(axis_size):
    near = [1 << t for t in range(axis_size.bit_length() - 1)]
    return near, near[1:2] + near[:1] + near[2:]


def places(order):
    bits = len(order)
    return [
        sum(((p >> (bits - 1 - t)) & 1) * order[t] for t in range(bits))
        for p in range(1 << bits)
    ]


def add_wide(left, right):
    return (left.astype(F32) + right.astype(F32)).astype(left.dtype)


class Reduce:
    def __init__(self, keep, send, axis, order):
        self.keep, self.send, self.axis, self.order = keep, send, axis, list(order)

    def step(self, after=()):
        got = swap(self.send, self.axis, self.order.pop(0))
        got = lax.optimization_barrier((got, after))[0]
        half = self.keep.shape[0] // 2
        if half == 0:
            self.keep, self.send = add_wide(self.keep[0], got[0]), None
        else:
            self.send = add_wide(self.keep[half:], got[half:])
            self.keep = add_wide(self.keep[:half], got[:half])

    def finish(self):
        while self.order:
            self.step()
        return self.keep


def send_direct(keep, send, axis, order):
    half = keep.shape[0]
    pieces = [keep[p] for p in range(half)] + [send[p] for p in range(half)]
    return [
        swap(piece, axis, mask) if mask else piece
        for piece, mask in zip(pieces, places(order))
    ]


class Gather:
    def __init__(self, x, axis, order):
        self.near, self.far, self.axis, self.order = x[None], None, axis, list(order)

    def step(self):
        if self.far is not None:
            self.near = jnp.concatenate([self.near, self.far], axis=0)
        self.far = swap(self.near, self.axis, self.order.pop())

    def finish(self):
        while self.order:
            self.step()
        return self.near, self.far


def hold(x, *chains):
    held = [(c.keep, c.send) if isinstance(c, Reduce) else (c.near, c.far) for c in chains]
    x, held = lax.optimization_barrier((x, held))
    for chain, state in zip(chains, held):
        if isinstance(chain, Reduce):
            chain.keep, chain.send = state
        else:
            chain.near, chain.far = state
    return x


def dot(left, right, dims=NN):
    return lax.dot_general(left, right, (dims, ((), ())), preferred_element_type=F32)


def parts(x, count):
    found = []
    for _ in range(count):
        term = x.astype(BF16)
        found.append(term)
        x = x - term.astype(F32)
    return found


def dot_fine(left, right, dims=NN):
    left_high, left_low = parts(left, 2)
    right_high, right_low = parts(right, 2)
    return (
        dot(left_high, right_high, dims)
        + dot(left_low, right_high, dims)
        + dot(left_high, right_low, dims)
    )


def dot_left(left, right, dims=NN, count=2):
    return sum(dot(term, right, dims) for term in parts(left, count))


def dot_right(left, right, dims=NN, count=2):
    return sum(dot(left, term, dims) for term in parts(right, count))


def silu(x):
    return x * jax.nn.sigmoid(x)


def silu_slope(inputs):
    sigma = jax.nn.sigmoid(inputs)
    return sigma * (1.0 + inputs * (1.0 - sigma))


def softplus(x):
    return jnp.maximum(x, 0.0) + jnp.log1p(jnp.exp(-jnp.abs(x)))


def iota(shape, dim):
    return lax.broadcasted_iota(jnp.int32, shape, dim)


def spread(heads, inner):
    lane, head = iota((heads, inner), 1), iota((heads, inner), 0)
    size = inner // heads
    inside = (lane >= head * size) & (lane < (head + 1) * size)
    return jnp.where(inside, 1.0, 0.0).astype(BF16)


def lane_blocks(heads, inner):
    size = inner // heads
    for start in range(0, inner, LANES):
        stop = min(start + LANES, inner)
        yield start, stop, range(start // size, stop // size)


def head_lanes(start, stop, head, size, length):
    lane = iota((length, stop - start), 1) + start
    return (lane >= head * size) & (lane < (head + 1) * size)


def local(body, outs, args, scratch=(), steps=1, flops=100_000_000):
    def spec(shape, dim, smem=False):
        if smem:
            return pl.BlockSpec(memory_space=pltpu.SMEM)
        block = [size // steps if at == dim else size for at, size in enumerate(shape)]
        return pl.BlockSpec(
            tuple(block),
            lambda step, dim=dim: tuple(step if at == dim else 0 for at in range(len(shape))),
        )

    pairs = [a if isinstance(a, tuple) else (a, None) for a in args]
    trio = [o if len(o) == 3 else (*o, None) for o in outs]
    size = sum(a.size * a.dtype.itemsize for a, _ in pairs)
    return pl.pallas_call(
        body,
        grid=(steps,),
        out_shape=[jax.ShapeDtypeStruct(shape, dtype) for shape, dtype, _ in trio],
        in_specs=[spec(a.shape, dim, a.dtype == jnp.int32) for a, dim in pairs],
        out_specs=[spec(shape, dim) for shape, _, dim in trio],
        scratch_shapes=list(scratch),
        compiler_params=pltpu.CompilerParams(vmem_limit_bytes=60 * 2**20),
        cost_estimate=pl.CostEstimate(
            flops=flops, bytes_accessed=size // 4, transcendentals=0
        ),
    )(*[a for a, _ in pairs])


def accumulate(ref, value):
    first = pl.program_id(0) == 0

    @pl.when(first)
    def _():
        ref[...] = value

    @pl.when(jnp.logical_not(first))
    def _():
        ref[...] += value


def as_row(ref):
    return ref[...].reshape(1, -1)


def as_column(row):
    count = row.shape[1]
    eye = iota((count, count), 0) == iota((count, count), 1)
    return jnp.sum(jnp.where(eye, row, 0.0), axis=1, keepdims=True)


def first_kernel(
    tokens_ref,
    edge_ref,
    gain_ref,
    value_proj_ref,
    state_proj_ref,
    step_proj_ref,
    conv_value_ref,
    conv_value_bias_ref,
    conv_state_ref,
    conv_state_bias_ref,
    step_bias_ref,
    decay_log_ref,
    normed_ref,
    value_in_ref,
    state_in_ref,
    values_ref,
    states_ref,
    value_slope_ref,
    state_slope_ref,
    step_x_ref,
    exp_cum_x_ref,
    end_x_ref,
    weighted_ref,
    cum_ref,
    cum_t_ref,
    step_arg_t_ref,
    ends_ref,
):
    _, length, _ = tokens_ref.shape
    inner = values_ref.shape[2]
    heads = cum_ref.shape[2]
    nstate = states_ref.shape[2] // 2
    blocks, share = ends_ref.shape[0], ends_ref.shape[1] - 8
    spread_mat = spread(heads, inner)
    row, col = iota((length, length), 0), iota((length, length), 1)
    lower = jnp.where(row >= col, 1.0, 0.0).astype(BF16)
    upper = jnp.where(row <= col, 1.0, 0.0).astype(BF16)
    step_bias = as_row(step_bias_ref)
    rate = jnp.exp(as_row(decay_log_ref))
    for source, first, count in ((edge_ref, 0, PAD), (tokens_ref, PAD, length)):
        x = source[0].astype(F32)
        scale = lax.rsqrt(jnp.mean(x * x, axis=-1, keepdims=True) + EPS)
        normed_ref[0, first : first + count] = (x * scale * as_row(gain_ref)).astype(BF16)
    normed = normed_ref[0, PAD:]
    step_arg = dot(normed, step_proj_ref[...], NT) + step_bias
    step_arg_t = dot(step_proj_ref[...], normed, NT) + as_column(step_bias)
    step_arg_t_ref[0] = step_arg_t
    step = softplus(step_arg)
    cum = dot_right(lower, -step * rate, NN, 3)
    cum_ref[0] = cum
    cum_t_ref[0] = dot_left(-softplus(step_arg_t) * as_column(rate), upper, NN, 3)
    step_x = dot_left(step, spread_mat)
    exp_cum_x = dot_left(jnp.exp(cum), spread_mat)
    end_x = dot_left(jnp.exp(cum[length - 1 :] - cum), spread_mat)
    step_x_ref[0] = step_x
    exp_cum_x_ref[0] = exp_cum_x
    end_x_ref[0] = end_x

    def convolve(proj_ref, weight_ref, bias_ref, in_ref, out_ref, slope_ref):
        taps = weight_ref.shape[0]
        in_ref[0] = dot(normed_ref[0], proj_ref[...])
        conv_out = as_row(bias_ref)
        for tap in range(taps):
            first = PAD - taps + 1 + tap
            conv_out = conv_out + weight_ref[tap : tap + 1] * in_ref[0, first : first + length]
        sigma = jax.nn.sigmoid(conv_out)
        slope_ref[0] = sigma * (1.0 + conv_out * (1.0 - sigma))
        out_ref[0] = conv_out * sigma

    convolve(
        state_proj_ref,
        conv_state_ref,
        conv_state_bias_ref,
        state_in_ref,
        states_ref,
        state_slope_ref,
    )
    convolve(
        value_proj_ref,
        conv_value_ref,
        conv_value_bias_ref,
        value_in_ref,
        values_ref,
        value_slope_ref,
    )
    weighted = end_x * step_x * values_ref[0]
    weighted_ref[0] = weighted
    ends = dot_fine(states_ref[0, :, :nstate], weighted, TN)
    for block in range(blocks):
        ends_ref[block, 0:8] = jnp.broadcast_to(exp_cum_x[length - 1 :], (8, inner))
        ends_ref[block, 8:] = ends[block * share : (block + 1) * share]


def scan_kernel(got_ref, entering_ref):
    running = jnp.zeros(entering_ref.shape[1:], F32)
    for block in range(got_ref.shape[0]):
        entering_ref[block] = running
        running = got_ref[block, 0:1] * running + got_ref[block, 8:]


def back_scan_kernel(got_ref, back_ref, leaving_ref):
    running = jnp.zeros(leaving_ref.shape[1:], F32)
    for block in reversed(range(got_ref.shape[0])):
        leaving_ref[block] = running
        running = got_ref[block, 0:1] * running + back_ref[block]


def inside_kernel(
    normed_ref,
    gate_proj_ref,
    values_ref,
    states_ref,
    step_x_ref,
    cum_ref,
    cum_t_ref,
    cot_ref,
    out_proj_ref,
    skip_ref,
    base_ref,
    gnorm_ref,
    gate_pre_ref,
):
    seqs, length, inner = base_ref.shape
    heads = cum_ref.shape[2]
    size = inner // heads
    nstate = states_ref.shape[2] // 2
    skip = dot_left(as_row(skip_ref), spread(heads, inner), NN, 3)
    causal = iota((length, length), 0) >= iota((length, length), 1)
    for seq in range(seqs):
        gate_pre_ref[seq] = dot(normed_ref[seq, PAD:], gate_proj_ref[...])
        products = dot_fine(states_ref[seq, :, nstate:], states_ref[seq, :, :nstate], NT)
        for start, stop, block_heads in lane_blocks(heads, inner):
            values = values_ref[seq, :, start:stop]
            scaled = parts(values * step_x_ref[seq, :, start:stop], 2)
            total = None
            for head in block_heads:
                gap = cum_ref[seq, :, head : head + 1] - cum_t_ref[seq, head : head + 1, :]
                decay = jnp.exp(jnp.where(causal, gap, -1e30))
                high, low = parts(decay * products, 2)
                part = dot(high, scaled[0]) + dot(low, scaled[0]) + dot(high, scaled[1])
                if total is None:
                    total = part
                else:
                    total = jnp.where(head_lanes(start, stop, head, size, length), part, total)
            base_ref[seq, :, start:stop] = total + skip[:, start:stop] * values
        gnorm_ref[seq] = dot(cot_ref[seq * length : (seq + 1) * length], out_proj_ref[...], NT)


def read_kernel(
    state_ref,
    states_ref,
    exp_cum_x_ref,
    base_ref,
    gate_pre_ref,
    gnorm_ref,
    out_gain_ref,
    read_ref,
    sums_ref,
):
    seqs, length, inner = base_ref.shape
    nstate = states_ref.shape[2] // 2
    ones = jnp.ones((8, inner), BF16)
    for seq in range(seqs):
        read = exp_cum_x_ref[seq] * dot_fine(states_ref[seq, :, nstate:], state_ref[seq])
        read_ref[seq] = read
        gated = (base_ref[seq] + read) * silu(gate_pre_ref[seq])
        squares = dot_right(ones, gated * gated, NT)
        backs = dot_right(ones, gnorm_ref[seq] * as_row(out_gain_ref) * gated, NT)
        row = iota((8, length), 0)
        sums_ref[:, seq * length : (seq + 1) * length] = jnp.where(row == 0, squares, backs)


def gate_kernel(
    sums_ref,
    read_ref,
    base_ref,
    gate_pre_ref,
    gnorm_ref,
    out_gain_ref,
    exp_cum_x_ref,
    states_ref,
    grad_scan_ref,
    back_ref,
    *,
    inner_total,
):
    nstate = states_ref.shape[2] // 2
    blocks, share = back_ref.shape[0], back_ref.shape[1]
    sums = jnp.transpose(sums_ref[...])
    scale = lax.rsqrt(sums[:, 0:1] / inner_total + EPS)
    back_mean = scale * sums[:, 1:2] / inner_total
    gate_act = silu(gate_pre_ref[0])
    unit = (base_ref[0] + read_ref[0]) * gate_act * scale
    grad_gated = scale * (gnorm_ref[0] * as_row(out_gain_ref) - unit * back_mean)
    grad_scan = grad_gated * gate_act
    grad_scan_ref[0] = grad_scan
    back = dot_fine(states_ref[0, :, nstate:], exp_cum_x_ref[0] * grad_scan, TN)
    for block in range(blocks):
        back_ref[block] = back[block * share : (block + 1) * share]


def cut_lines(held, value):
    count = held.shape[1]
    for piece in range(held.shape[0]):
        held[piece] = value[piece * count : (piece + 1) * count]


def stacked(lines, lanes):
    return [lines[:, at : at + lanes] for at in range(0, lines.shape[1], lanes)]


def ordered_piece(own, at, value, keep_ref, send_ref):
    half = keep_ref.shape[0]
    for p, mask in enumerate(places(orders(2 * half)[0])):

        @pl.when((own ^ mask) == at)
        def _():
            (keep_ref if p < half else send_ref)[p % half, :, : value.shape[1]] = value


def low_kernel(
    own_ref,
    sums_ref,
    read_ref,
    base_ref,
    gate_pre_ref,
    gnorm_ref,
    out_gain_ref,
    grad_scan_ref,
    values_ref,
    normed_ref,
    cot_ref,
    out_proj_ref,
    proj_ref,
    grad_gate_ref,
    rows_ref,
    gain_row_ref,
    keep_ref,
    send_ref,
    branch_keep_ref,
    branch_send_ref,
    gate_low,
    grad_gate_proj,
    grad_out_proj,
    *,
    inner_total,
):
    seqs, length, inner = base_ref.shape
    gain_sum = jnp.zeros((1, inner), F32)
    skip_sum = jnp.zeros((1, inner), F32)
    pieces = 2 * branch_keep_ref.shape[0]
    col_width = branch_keep_ref.shape[2]
    total = None
    for seq in range(seqs):
        sums = jnp.transpose(sums_ref[:, seq * length : (seq + 1) * length])
        scale = lax.rsqrt(sums[:, 0:1] / inner_total + EPS)
        back_mean = scale * sums[:, 1:2] / inner_total
        gate_pre = gate_pre_ref[seq]
        sigma = jax.nn.sigmoid(gate_pre)
        scan_out = base_ref[seq] + read_ref[seq]
        unit = scan_out * gate_pre * sigma * scale
        gnorm = gnorm_ref[seq]
        gate_low[seq * length : (seq + 1) * length] = (unit * as_row(out_gain_ref)).astype(BF16)
        grad_gated = scale * (gnorm * as_row(out_gain_ref) - unit * back_mean)
        slope = sigma * (1.0 + gate_pre * (1.0 - sigma))
        grad_gate = (grad_gated * scan_out * slope).astype(BF16)
        grad_gate_ref[seq] = grad_gate
        part = dot(normed_ref[seq, PAD:], grad_gate, TN)
        total = part if total is None else total + part
        gain_sum = gain_sum + jnp.sum(gnorm * unit, axis=0, keepdims=True)
        skip_sum = skip_sum + jnp.sum(
            grad_scan_ref[seq] * values_ref[seq], axis=0, keepdims=True
        )
    rows_ref[:, :inner] = gain_sum
    rows_ref[:, inner:] = skip_sum
    ones = jnp.ones((8, inner), BF16)
    gain_row_ref[...] = dot_right(ones, total * proj_ref[...].astype(F32), NT)
    cut_lines(grad_gate_proj, total)
    cut_lines(grad_out_proj, dot(gate_low[...], cot_ref[...], TN))
    blocks = 2 * keep_ref.shape[0]
    for p, mask in enumerate(places(orders(blocks)[0])):
        at = own_ref[0] ^ mask
        ref = keep_ref if p < blocks // 2 else send_ref
        value = jnp.concatenate(
            [grad_gate_proj[at], *stacked(grad_out_proj[at], inner)], axis=0
        )
        ref[p % (blocks // 2)] = value.astype(BF16)
    branch = dot(gate_low[...], out_proj_ref[...])
    for piece in range(pieces):
        value = branch[:, piece * col_width : (piece + 1) * col_width].astype(BF16)
        ordered_piece(own_ref[1], piece, value, branch_keep_ref, branch_send_ref)


def mix_kernel(
    values_ref,
    states_ref,
    step_x_ref,
    exp_cum_x_ref,
    cum_ref,
    cum_t_ref,
    grad_scan_ref,
    state_ref,
    scaled_grad_ref,
    grad_b_ref,
    grad_c_ref,
    gaps_ref,
):
    seqs, length, inner = grad_scan_ref.shape
    heads = cum_ref.shape[2]
    size = inner // heads
    nstate = states_ref.shape[2] // 2
    causal = iota((length, length), 0) >= iota((length, length), 1)
    ones = jnp.ones((8, length), BF16)
    for seq in range(seqs):
        b_rows = states_ref[seq, :, :nstate]
        c_rows = states_ref[seq, :, nstate:]
        products = dot_fine(c_rows, b_rows, NT)
        grad_products = jnp.zeros((length, length), F32)
        for start, stop, block_heads in lane_blocks(heads, inner):
            scaled = values_ref[seq, :, start:stop] * step_x_ref[seq, :, start:stop]
            scaled_high, scaled_low = parts(scaled, 2)
            scan_high, scan_low = parts(grad_scan_ref[seq, :, start:stop], 2)
            total = None
            for head in block_heads:
                gap = cum_ref[seq, :, head : head + 1] - cum_t_ref[seq, head : head + 1, :]
                decay = jnp.exp(jnp.where(causal, gap, -1e30))
                own = head_lanes(start, stop, head, size, length)
                own_high = jnp.where(own, scan_high, jnp.zeros_like(scan_high))
                own_low = jnp.where(own, scan_low, jnp.zeros_like(scan_low))
                grad_mix = (
                    dot(own_high, scaled_high, NT)
                    + dot(own_low, scaled_high, NT)
                    + dot(own_high, scaled_low, NT)
                )
                grad_decayed = grad_mix * decay
                grad_products = grad_products + grad_decayed
                related = (grad_decayed * products).astype(BF16)
                gaps = dot(ones, related, NT) - dot(ones, related)
                gaps_ref[seq, head : head + 1] = gaps[0:1]
                part = dot((decay * products).astype(BF16), own_high, TN)
                total = part if total is None else total + part
            scaled_grad_ref[seq, :, start:stop] = total
        carried = exp_cum_x_ref[seq] * grad_scan_ref[seq]
        grad_c_ref[seq] = dot_fine(grad_products, b_rows) + dot_fine(
            carried, state_ref[seq], NT
        )
        grad_b_ref[seq] = dot_fine(grad_products, c_rows, TN)


def state_sum_kernel(
    own_ref,
    grad_end_ref,
    weighted_ref,
    grad_b_ref,
    grad_c_ref,
    keep_ref,
    send_ref,
):
    pieces, part = 2 * keep_ref.shape[0], keep_ref.shape[2]
    grad_b = grad_b_ref[0] + dot_fine(weighted_ref[0], grad_end_ref[0], NT)
    both = jnp.concatenate([grad_b, grad_c_ref[0]], axis=1)
    for piece in range(pieces):
        value = both[:, piece * part : (piece + 1) * part]
        ordered_piece(own_ref[1], piece, value, keep_ref, send_ref)


def conv_back(grad_out, in_ref, weight_ref, seq, around):
    length = grad_out.shape[0]
    taps = weight_ref.shape[0]
    around[PAD : PAD + length] = grad_out
    grad_in = None
    sums = []
    for tap in range(taps):
        first = PAD - taps + 1 + tap
        sums.append(
            jnp.sum(grad_out * in_ref[seq, first : first + length], axis=0, keepdims=True)
        )
        first = taps - 1 - tap
        part = weight_ref[tap : tap + 1] * around[first : first + PAD + length]
        grad_in = part if grad_in is None else grad_in + part
    sums.append(jnp.sum(grad_out, axis=0, keepdims=True))
    return grad_in, jnp.concatenate(sums, axis=0)


def clear_edges(around):
    zeros = jnp.zeros((PAD, around.shape[1]), F32)
    around[0:PAD] = zeros
    around[around.shape[0] - PAD :] = zeros


def value_kernel(
    grad_end_ref,
    state_ref,
    values_ref,
    states_ref,
    slope_ref,
    conv_in_ref,
    conv_weight_ref,
    step_x_ref,
    exp_cum_x_ref,
    end_x_ref,
    step_arg_t_ref,
    decay_log_ref,
    skip_ref,
    read_ref,
    grad_scan_ref,
    scaled_grad_ref,
    gaps_ref,
    grad_in_ref,
    grad_step_t_ref,
    conv_rows_ref,
    head_rows_ref,
    around,
):
    _, length, inner = values_ref.shape
    heads = gaps_ref.shape[1]
    nstate = states_ref.shape[2] // 2
    spread_mat = spread(heads, inner)
    row, col = iota((length, length), 0), iota((length, length), 1)
    lower = jnp.where(row >= col, 1.0, 0.0).astype(BF16)
    rate_t = as_column(jnp.exp(as_row(decay_log_ref)))
    skip = dot_left(as_row(skip_ref), spread_mat, NN, 3)
    last = iota((heads, length), 1) == length - 1
    clear_edges(around)
    values = values_ref[0]
    grad_end = grad_end_ref[0]
    step_x = step_x_ref[0]
    grad_scan = grad_scan_ref[0]
    end_proj = end_x_ref[0] * dot(
        states_ref[0, :, :nstate].astype(BF16), grad_end.astype(BF16)
    )
    scaled_grad = scaled_grad_ref[0] + end_proj
    grad_in, conv_rows = conv_back(
        (skip * grad_scan + step_x * scaled_grad) * slope_ref[0],
        conv_in_ref,
        conv_weight_ref,
        0,
        around,
    )
    grad_in_ref[0] = grad_in
    end_terms = dot_right(spread_mat, step_x * values * end_proj, NT)
    crossed = jnp.sum(grad_end * state_ref[0], axis=0, keepdims=True)
    crossed = crossed * exp_cum_x_ref[0, length - 1 :]
    last_term = jnp.sum(end_terms, axis=1, keepdims=True) + jnp.sum(
        jnp.where(spread_mat.astype(F32) > 0.0, crossed, 0.0), axis=1, keepdims=True
    )
    grad_cum = (
        gaps_ref[0] + dot_right(spread_mat, grad_scan * read_ref[0], NT) - end_terms
    ) + jnp.where(last, last_term, 0.0)
    grad_log = dot_left(grad_cum, lower, NN, 3)
    step_arg = step_arg_t_ref[0]
    rate_sum = -jnp.sum(grad_log * softplus(step_arg), axis=1, keepdims=True)
    grad_step = dot_right(spread_mat, values * scaled_grad, NT) - grad_log * rate_t
    grad_step = grad_step * jax.nn.sigmoid(step_arg)
    bias_sum = jnp.sum(grad_step, axis=1, keepdims=True)
    grad_step_t_ref[0] = grad_step.astype(BF16)
    lane = iota((heads, LANES), 1)
    accumulate(conv_rows_ref, conv_rows)
    accumulate(head_rows_ref, jnp.where(lane == 0, bias_sum, rate_sum * rate_t))


def small_places(heads, taps, lanes):
    return lanes - LANES, heads + max(heads, taps)


def weight_kernel(
    own_ref,
    normed_ref,
    value_in_ref,
    grad_step_t_ref,
    state_grad_ref,
    slope_ref,
    conv_in_ref,
    conv_weight_ref,
    gain_ref,
    gate_gain_row_ref,
    value_proj_ref,
    state_proj_t_ref,
    step_proj_t_ref,
    value_rows_ref,
    head_rows_ref,
    inner_row_ref,
    state_in_ref,
    keep_ref,
    send_ref,
    around,
    small,
    slope,
    conv_in,
    conv_weight,
    late,
    *,
    pieces,
):
    seqs, length, part = slope.shape
    for piece in range(pieces):

        @pl.when(own_ref[1] == piece)
        def _():
            lanes = slice(piece * part, (piece + 1) * part)
            slope[...] = slope_ref[:, :, lanes]
            conv_in[...] = conv_in_ref[:, :, lanes]
            conv_weight[...] = conv_weight_ref[:, lanes]

    width = normed_ref.shape[2]
    blocks, _, inner = late.shape
    value_total = state_total = step_total = conv_total = None

    def add(total, part):
        return part if total is None else total + part

    clear_edges(around)
    for seq in range(seqs):
        normed = normed_ref[seq]
        grad = state_grad_ref[seq * length : (seq + 1) * length] * slope[seq]
        grad_in, conv_rows = conv_back(grad, conv_in, conv_weight, seq, around)
        state_in_ref[seq] = grad_in
        conv_total = add(conv_total, conv_rows)
        value_total = add(value_total, dot(normed, value_in_ref[seq].astype(BF16), TN))
        state_total = add(state_total, dot(grad_in.astype(BF16), normed, TN))
        step_total = add(step_total, dot(grad_step_t_ref[seq], normed_ref[seq, PAD:]))
    ones = jnp.ones((8, inner), BF16)
    gain_row = gate_gain_row_ref[...] + dot_right(
        ones, value_total * value_proj_ref[...].astype(F32), NT
    )
    gain_row = (
        gain_row[0:1]
        + jnp.sum(state_total * state_proj_t_ref[...].astype(F32), axis=0, keepdims=True)
        + jnp.sum(step_total * step_proj_t_ref[...].astype(F32), axis=0, keepdims=True)
    )
    heads, taps = step_total.shape[0], value_rows_ref.shape[0]
    heads_at, last = small_places(heads, taps, small.shape[1])
    small[...] = jnp.zeros(small.shape, F32)
    small[:heads, :width] = step_total
    small[heads : heads + taps, :inner] = value_rows_ref[...]
    for piece in range(pieces):

        @pl.when(own_ref[1] == piece)
        def _():
            first = inner + piece * part
            small[heads : heads + taps, first : first + part] = conv_total

    small[heads : 2 * heads, heads_at:] = head_rows_ref[...]
    small[last : last + 1, : 2 * inner] = inner_row_ref[...]
    small[last + 1 : last + 2, :width] = gain_row / as_row(gain_ref)
    small_rows = jnp.concatenate(stacked(small[...], inner), axis=0)
    small_lines = small_rows.shape[0] // blocks
    value_lines = width // blocks
    state_lines = state_total.shape[0] // blocks
    for block in range(blocks):
        value = value_total[block * value_lines : (block + 1) * value_lines]
        state = state_total[block * state_lines : (block + 1) * state_lines]
        lines = small_rows[block * small_lines : (block + 1) * small_lines]
        value = [value, *stacked(state, inner), *[x.astype(F32) for x in parts(lines, 2)]]
        spare = late.shape[1] - sum(x.shape[0] for x in value)
        if spare:
            value.append(jnp.zeros((spare, inner), F32))
        late[block] = jnp.concatenate(value, axis=0).astype(BF16)
    for p, mask in enumerate(places(orders(blocks)[0])):
        ref = keep_ref if p < blocks // 2 else send_ref
        ref[p % (blocks // 2)] = late[own_ref[0] ^ mask]


def sum_terms(terms, first, lines):
    total = terms[0].astype(F32)
    for term in terms[1:]:
        total = total + term.astype(F32)
    small = total[first : first + lines] + total[first + lines : first + 2 * lines]
    small = [x.astype(F32) for x in parts(small, 2)]
    spare = [total[first + 2 * lines :]] if total.shape[0] > first + 2 * lines else []
    return jnp.concatenate([total[:first], *small, *spare], axis=0).astype(BF16)


def pair_kernel(keep_ref, got_ref, out_ref, **small):
    for block in range(out_ref.shape[0]):
        out_ref[block] = sum_terms([keep_ref[block], got_ref[block]], **small)


def sum_kernel(*refs, **small):
    total = sum_terms([ref[...] for ref in refs[:-1]], **small)
    for block in range(refs[-1].shape[0]):
        refs[-1][block] = total


def place_kernel(own_ref, near_ref, far_ref, gate_ref, out_ref):
    blocks, lines, inner = gate_ref.shape
    count = out_ref.shape[1]
    for p, mask in enumerate(places(orders(blocks)[0])):
        ref = near_ref if p < blocks // 2 else far_ref
        value = ref[p % (blocks // 2)].astype(F32)
        at = own_ref[0] ^ mask
        gate_ref[at] = value[:lines]
        for group in range(out_ref.shape[2] // inner):
            first = lines + group * count
            out_ref[at, :, group * inner : (group + 1) * inner] = value[first : first + count]


def back_kernel(
    own_ref,
    tokens_ref,
    gain_ref,
    value_in_ref,
    state_in_ref,
    value_over_ref,
    state_over_ref,
    value_proj_ref,
    state_proj_t_ref,
    grad_gate_ref,
    gate_proj_ref,
    grad_step_t_ref,
    step_proj_t_ref,
    keep_ref,
    send_ref,
    *,
    col_width,
):
    _, length, width = tokens_ref.shape
    pieces = 2 * keep_ref.shape[0]
    def whole(in_ref, over_ref, seq):
        return jnp.concatenate(
            [
                in_ref[seq, PAD:length].astype(BF16),
                (in_ref[seq, length:] + over_ref[seq]).astype(BF16),
            ],
            axis=0,
        )

    x = tokens_ref[0].astype(F32)
    unit = x * lax.rsqrt(jnp.mean(x * x, axis=-1, keepdims=True) + EPS)
    normed_grad = (
        dot(whole(value_in_ref, value_over_ref, 0), value_proj_ref[...], NT)
        + dot(whole(state_in_ref, state_over_ref, 0), state_proj_t_ref[...])
        + dot(grad_gate_ref[0], gate_proj_ref[...], NT)
        + dot(grad_step_t_ref[0], step_proj_t_ref[...], TN)
    )
    unit_grad = normed_grad * as_row(gain_ref)
    row_sum = jnp.sum(unit_grad * unit, axis=-1, keepdims=True).astype(BF16)
    row_sum = jnp.broadcast_to(row_sum, (length, LANES))
    for half_ref in (keep_ref, send_ref):
        for p in range(pieces // 2):
            half_ref[p, :, half_ref.shape[2] - LANES :] = row_sum
    for piece in range(pieces):
        value = unit_grad[:, piece * col_width : (piece + 1) * col_width].astype(BF16)
        ordered_piece(own_ref[1], piece, value, keep_ref, send_ref)


def last_kernel(
    own_ref,
    near_ref,
    far_ref,
    state_proj_ref,
    norm_gain_ref,
    step_proj_ref,
    conv_value_ref,
    conv_value_bias_ref,
    conv_state_ref,
    conv_state_bias_ref,
    step_bias_ref,
    decay_log_ref,
    skip_gain_ref,
    out_gain_ref,
    held,
    smalls,
):
    half, blocks, _, inner = near_ref.shape
    pieces, _, each, width = held.shape
    _, lines, lanes = smalls.shape
    state_lines = each * width // inner
    small_lines = lines * lanes // inner // blocks
    for p, mask in enumerate(places(orders(2 * half)[0])):
        ref = near_ref if p < half else far_ref
        at = own_ref[1] ^ mask
        small = []
        for block in range(blocks):
            value = ref[p % half, block].astype(F32)
            for group in range(width // inner):
                held[at, block, :, group * inner : (group + 1) * inner] = value[
                    group * each : (group + 1) * each
                ]
            high = value[state_lines : state_lines + small_lines]
            small.append(high + value[state_lines + small_lines : state_lines + 2 * small_lines])
        small = jnp.concatenate(small, axis=0)
        smalls[at] = jnp.concatenate(
            [small[first : first + lines] for first in range(0, small.shape[0], lines)], axis=1
        )
    state_proj_ref[...] = jnp.transpose(held[...].reshape(-1, width))
    whole = smalls[0]
    for piece in range(1, pieces):
        whole = whole + smalls[piece]
    small = smalls[own_ref[1]]
    heads = step_proj_ref.shape[0]
    taps = conv_value_ref.shape[0]
    channels = inner + conv_state_ref.shape[1]
    heads_at, last = small_places(heads, taps + 1, lanes)
    norm_gain_ref[...] = whole[last + 1, :width]
    step_proj_ref[...] = small[:heads, :width]
    conv_value_ref[...] = small[heads : heads + taps, :inner]
    conv_value_bias_ref[...] = small[heads + taps, :inner]
    conv_state_ref[...] = whole[heads : heads + taps, inner:channels]
    conv_state_bias_ref[...] = whole[heads + taps, inner:channels]
    sums = small[heads : 2 * heads, heads_at : heads_at + 2]
    eye = iota((heads, heads), 0) == iota((heads, heads), 1)
    step_bias_ref[...] = jnp.sum(jnp.where(eye, sums[:, 0:1], 0.0), axis=0)
    decay_log_ref[...] = jnp.sum(jnp.where(eye, sums[:, 1:2], 0.0), axis=0)
    row = small[last : last + 1, : 2 * inner]
    out_gain_ref[...] = row[0, :inner]
    skip = dot_left(row[:, inner:], spread(heads, inner), NT, 3)
    skip_gain_ref[...] = skip.reshape(heads)


def on_device(
    tokens,
    norm_gain,
    gate_proj,
    value_proj,
    state_proj,
    step_proj,
    conv_value,
    conv_value_bias,
    conv_state,
    conv_state_bias,
    step_bias,
    decay_log,
    skip_gain,
    out_gain,
    out_proj,
    cotangent,
):
    seqs, length, width = tokens.shape
    rows = seqs * length
    heads = step_proj.shape[1]
    inner = gate_proj.shape[1]
    head_dim = inner // heads
    nstate = state_proj.shape[1] // 2
    taps = conv_value.shape[0]
    channels = inner + 2 * nstate
    head_devices = lax.axis_size("head")
    blocks = lax.axis_size("seq")
    head_index = lax.axis_index("head")
    own = jnp.stack([lax.axis_index("seq"), head_index]).astype(jnp.int32)
    col_width = width // head_devices
    share = seqs * nstate // blocks
    part = 2 * nstate // head_devices
    full = (seqs, length, inner)
    inner_total = inner * head_devices

    def own_cols(x, size):
        return lax.dynamic_slice_in_dim(x, head_index * size, size, x.ndim - 1)

    def cut(*arrays):
        return [(x, 0) for x in arrays]

    edge_tokens = shift(tokens[:, length - PAD :, :], "seq", 1)
    step_proj_t = jnp.transpose(step_proj)
    state_proj_t = jnp.transpose(state_proj)
    state_proj_t = lax.dynamic_slice_in_dim(state_proj_t, head_index * part, part, 0)
    (
        normed,
        value_conv_in,
        state_conv_in,
        values,
        states,
        value_slope,
        state_slope,
        step_x,
        exp_cum_x,
        end_x,
        weighted,
        cum,
        cum_t,
        step_arg_t,
        ends,
    ) = local(
        first_kernel,
        [
            ((seqs, PAD + length, width), BF16, 0),
            ((seqs, PAD + length, inner), F32, 0),
            ((seqs, PAD + length, 2 * nstate), F32, 0),
            (full, F32, 0),
            ((seqs, length, 2 * nstate), F32, 0),
            (full, F32, 0),
            ((seqs, length, 2 * nstate), F32, 0),
            (full, F32, 0),
            (full, F32, 0),
            (full, F32, 0),
            (full, F32, 0),
            ((seqs, length, heads), F32, 0),
            ((seqs, heads, length), F32, 0),
            ((seqs, heads, length), F32, 0),
            ((blocks, 8 + share, inner), F32, 0),
        ],
        [
            *cut(tokens, edge_tokens),
            norm_gain,
            value_proj,
            state_proj,
            step_proj_t,
            conv_value,
            conv_value_bias,
            conv_state,
            conv_state_bias,
            step_bias,
            decay_log,
        ],
        steps=seqs,
    )
    got = lax.all_to_all(ends, "seq", 0, 0)
    cot_rows = cotangent.reshape(rows, col_width)
    cot_low, _ = lax.optimization_barrier((cot_rows.astype(BF16), ends))
    cot_low = lax.all_gather(cot_low, "head", axis=1, tiled=True)
    got, cot_low = lax.optimization_barrier((got, cot_low))
    (entering,) = local(scan_kernel, [((blocks, share, inner), F32)], [got])
    state_in = lax.all_to_all(entering, "seq", 0, 0).reshape(seqs, nstate, inner)
    base, gnorm, gate_pre = local(
        inside_kernel,
        [(full, F32, 0), (full, F32, 0), (full, F32, 0)],
        [
            (normed, 0),
            gate_proj,
            *cut(values, states, step_x, cum, cum_t, cot_low),
            out_proj,
            skip_gain,
        ],
        steps=seqs,
    )
    read, row_sums = local(
        read_kernel,
        [(full, F32, 0), ((8, rows), F32, 1)],
        [*cut(state_in, states, exp_cum_x, base, gate_pre, gnorm), out_gain],
        steps=seqs,
    )
    row_sums = sum_all(row_sums, "head")
    grad_scan, back = local(
        functools.partial(gate_kernel, inner_total=inner_total),
        [(full, F32, 0), ((blocks, share, inner), F32, 0)],
        [
            (row_sums, 1),
            *cut(read, base, gate_pre, gnorm),
            out_gain,
            *cut(exp_cum_x, states),
        ],
        steps=seqs,
    )
    got_back = lax.all_to_all(back, "seq", 0, 0)

    def halves(axis_size, lines, lanes, dtype=BF16, dim=None):
        return [((axis_size // 2, lines, lanes), dtype, dim)] * 2

    (
        grad_gate,
        inner_row,
        gate_gain_row,
        early_keep,
        early_send,
        branch_keep,
        branch_send,
    ) = local(
        functools.partial(low_kernel, inner_total=inner_total),
        [
            (full, BF16),
            ((1, 2 * inner), F32),
            ((8, width), F32),
            *halves(blocks, 2 * (width // blocks), inner),
            *halves(head_devices, rows, col_width),
        ],
        [
            own,
            row_sums,
            read,
            base,
            gate_pre,
            gnorm,
            out_gain,
            grad_scan,
            values,
            normed,
            cot_low,
            out_proj,
            gate_proj,
        ],
        [
            pltpu.VMEM((rows, inner), BF16),
            pltpu.VMEM((blocks, width // blocks, inner), F32),
            pltpu.VMEM((blocks, inner // blocks, width), F32),
        ],
    )

    got_back = lax.optimization_barrier((got_back, early_send))[0]
    (leaving,) = local(back_scan_kernel, [((blocks, share, inner), F32)], [got, got_back])
    grad_end = lax.all_to_all(leaving, "seq", 0, 0).reshape(seqs, nstate, inner)
    near = orders(blocks)[0]
    near_head = orders(head_devices)[0]
    even = places(near)[: blocks // 2]
    branch_chain = Reduce(branch_keep, branch_send, "head", near_head)
    grad_scan = lax.optimization_barrier((grad_scan, leaving))[0]
    scaled_grad, grad_b, grad_c, gaps = local(
        mix_kernel,
        [
            (full, F32, 0),
            ((seqs, length, nstate), F32, 0),
            ((seqs, length, nstate), F32, 0),
            ((seqs, heads, length), F32, 0),
        ],
        cut(values, states, step_x, exp_cum_x, cum, cum_t, grad_scan, state_in),
        steps=seqs,
    )
    early = lax.optimization_barrier((swap(early_send, "seq", 1), gaps))[0]
    early = add_wide(early_keep, early)
    grad_end, early = lax.optimization_barrier((grad_end, early))
    early = [
        swap(early[p], "seq", mask) if mask else early[p] for p, mask in enumerate(even)
    ]
    state_keep, state_send = local(
        state_sum_kernel,
        halves(head_devices, rows, part, F32, 1),
        [own, *cut(grad_end, weighted, grad_b, grad_c)],
        steps=seqs,
    )
    state_part = send_direct(state_keep, state_send, "head", near_head)
    state_part = sum(state_part[1:], state_part[0])
    value_in, grad_step_t, value_rows, head_rows = local(
        value_kernel,
        [
            ((seqs, PAD + length, inner), F32, 0),
            ((seqs, heads, length), BF16, 0),
            ((taps + 1, inner), F32),
            ((heads, LANES), F32),
        ],
        [
            *cut(grad_end, state_in, values, states, value_slope, value_conv_in),
            conv_value,
            *cut(step_x, exp_cum_x, end_x, step_arg_t),
            decay_log,
            skip_gain,
            *cut(read, grad_scan, scaled_grad, gaps),
        ],
        [pltpu.VMEM((length + 2 * PAD, inner), F32)],
        steps=seqs,
    )
    value_lines = width // blocks
    state_lines = part // blocks * (width // inner)
    small_lanes = max(width, channels + LANES)
    small_rows = -(-(heads + max(heads, taps + 1) + 2) // 8) * 8
    small_lines = small_rows * (small_lanes // inner) // blocks
    late_lines = -(-(value_lines + state_lines + 2 * small_lines) // 16) * 16
    state_grad_in, late_keep, late_send = local(
        functools.partial(weight_kernel, pieces=head_devices),
        [
            ((seqs, PAD + length, part), F32),
            *halves(blocks, late_lines, inner),
        ],
        [
            own,
            normed,
            value_in,
            grad_step_t,
            state_part,
            state_slope,
            state_conv_in,
            conv_state,
            norm_gain,
            gate_gain_row,
            value_proj,
            state_proj_t,
            step_proj_t,
            value_rows,
            head_rows,
            inner_row,
        ],
        [
            pltpu.VMEM((length + 2 * PAD, part), F32),
            pltpu.VMEM((small_rows, small_lanes), F32),
            pltpu.VMEM((seqs, length, part), F32),
            pltpu.VMEM((seqs, PAD + length, part), F32),
            pltpu.VMEM((taps, part), F32),
            pltpu.VMEM((blocks, late_lines, inner), BF16),
        ],
    )
    late_send, early = lax.optimization_barrier((late_send, early))
    late = swap(late_send, "seq", 1)
    early = sum(x.astype(F32) for x in early).astype(BF16)
    early = [swap(early, "seq", mask) if mask else early for mask in even]
    late_small = dict(first=value_lines + state_lines, lines=small_lines)
    (late,) = local(
        functools.partial(pair_kernel, **late_small),
        [((blocks // 2, late_lines, inner), BF16)],
        [late_keep, late],
    )
    late = [swap(late[p], "seq", mask) if mask else late[p] for p, mask in enumerate(even)]
    over = jnp.concatenate([value_in[:, :PAD], state_grad_in[:, :PAD]], axis=2)
    over = shift(over, "seq", -1)
    own_source = own_cols(tokens.reshape(rows, width), col_width).astype(F32)
    back_width = -(-(col_width + 1) // LANES) * LANES
    keep, send = local(
        functools.partial(back_kernel, col_width=col_width),
        [
            *halves(head_devices, rows, back_width, BF16, 1),
        ],
        [
            own,
            (tokens, 0),
            norm_gain,
            *cut(value_in, state_grad_in, over[:, :, :inner], over[:, :, inner:]),
            value_proj,
            state_proj_t,
            (grad_gate, 0),
            gate_proj,
            (grad_step_t, 0),
            step_proj_t,
        ],
        steps=seqs,
    )
    branch_chain.step()
    branch_chain.step(after=(keep,))
    branch = branch_chain.finish().astype(F32)
    mixed_rows = jnp.swapaxes((own_source + branch).reshape(seqs, length, col_width), 1, 2)
    early = jnp.stack(early)
    late, mixed_rows, early, keep, send = lax.optimization_barrier(
        (late, mixed_rows, early, keep, send)
    )
    early_far = swap(early, "seq", 1)
    (late_values,) = local(
        functools.partial(sum_kernel, **late_small),
        [((blocks, late_lines, inner), BF16)],
        late,
    )
    late = lax.all_to_all(late_values, "seq", 0, 0)
    own_part = send_direct(keep, send, "head", near_head)
    own_part = sum(x.astype(F32) for x in own_part)
    row_mean = own_part[:, back_width - 1 :] / width
    own_part = own_part[:, :col_width]
    source = tokens.reshape(rows, width).astype(F32)
    own_scale = lax.rsqrt(jnp.mean(source * source, axis=-1, keepdims=True) + EPS)
    own_unit = own_source * own_scale
    grad_tokens = cot_rows + own_scale * (own_part - own_unit * row_mean)
    grad_tokens = jnp.swapaxes(grad_tokens.reshape(seqs, length, col_width), 1, 2)
    late, grad_tokens = lax.optimization_barrier((late, grad_tokens))
    grad_value_proj = late[:, :value_lines].reshape(width, inner).astype(F32)
    grad_gate_proj, grad_out_proj = local(
        place_kernel,
        [
            ((blocks, value_lines, inner), F32),
            ((blocks, inner // blocks, width), F32),
        ],
        [own, early, early_far],
    )
    grad_gate_proj = grad_gate_proj.reshape(width, inner)
    grad_out_proj = grad_out_proj.reshape(inner, width)
    state_chain = Gather(late[:, value_lines:], "head", near_head)
    state_chain.step()
    done = (grad_gate_proj, grad_out_proj, mixed_rows, grad_tokens)
    grad_gate_proj, grad_out_proj, mixed_rows, grad_tokens = hold(done, state_chain)
    (
        grad_state_proj,
        grad_norm_gain,
        grad_step_proj,
        grad_conv_value,
        grad_conv_value_bias,
        grad_conv_state,
        grad_conv_state_bias,
        grad_step_bias,
        grad_decay_log,
        grad_skip_gain,
        grad_out_gain,
    ) = local(
        last_kernel,
        [
            ((width, 2 * nstate), F32),
            ((width,), F32),
            ((heads, width), F32),
            ((taps, inner), F32),
            ((inner,), F32),
            ((taps, 2 * nstate), F32),
            ((2 * nstate,), F32),
            ((heads,), F32),
            ((heads,), F32),
            ((heads,), F32),
            ((inner,), F32),
        ],
        [own, *state_chain.finish()],
        [
            pltpu.VMEM((head_devices, blocks, part // blocks, width), F32),
            pltpu.VMEM((head_devices, small_rows, small_lanes), F32),
        ],
    )
    return (
        jnp.swapaxes(mixed_rows, 1, 2),
        jnp.swapaxes(grad_tokens, 1, 2),
        grad_norm_gain,
        grad_gate_proj,
        grad_value_proj,
        grad_state_proj,
        jnp.transpose(grad_step_proj),
        grad_conv_value,
        grad_conv_value_bias,
        grad_conv_state,
        grad_conv_state_bias,
        grad_step_bias,
        grad_decay_log,
        grad_skip_gain,
        grad_out_gain,
        grad_out_proj,
    )


def solution(mesh):
    return jax.shard_map(
        on_device,
        mesh=mesh,
        in_specs=(
            P(None, "seq", None),
            P(),
            P(None, "head"),
            P(None, "head"),
            P(),
            P(None, "head"),
            P(None, "head"),
            P("head"),
            P(),
            P(),
            P("head"),
            P("head"),
            P("head"),
            P("head"),
            P("head", None),
            P(None, "seq", "head"),
        ),
        out_specs=(
            P(None, "seq", "head"),
            P(None, "seq", "head"),
            P(),
            P(None, "head"),
            P(None, "head"),
            P(),
            P(None, "head"),
            P(None, "head"),
            P("head"),
            P(),
            P(),
            P("head"),
            P("head"),
            P("head"),
            P("head"),
            P("head", None),
        ),
        check_vma=False,
    )
```

```python
import functools

import jax
import jax.numpy as jnp
from jax import lax
from jax.experimental import pallas as pl
from jax.experimental.pallas import tpu as pltpu
from jax.sharding import PartitionSpec as P

EPS = 1e-05
F32 = jnp.float32
BF16 = jnp.bfloat16
NN = ((1,), (0,))
NT = ((1,), (1,))
TN = ((0,), (0,))
PAD = 16
LANES = 128


def shift(x, axis, by):
    devices = lax.axis_size(axis)
    pairs = [(i, i + by) for i in range(devices) if 0 <= i + by < devices]
    return lax.ppermute(x, axis, pairs)


def swap(x, axis, mask):
    devices = lax.axis_size(axis)
    return lax.ppermute(x, axis, [(i, i ^ mask) for i in range(devices)])


def masks(axis):
    found, mask = [], 1
    while mask < lax.axis_size(axis):
        found.append(mask)
        mask *= 2
    return found


def sum_all(x, axis):
    for mask in masks(axis):
        x = x + swap(x, axis, mask)
    return x


def orders(axis_size):
    near = [1 << t for t in range(axis_size.bit_length() - 1)]
    return near, near[1:2] + near[:1] + near[2:]


def places(order):
    bits = len(order)
    return [
        sum(((p >> (bits - 1 - t)) & 1) * order[t] for t in range(bits))
        for p in range(1 << bits)
    ]


def add_wide(left, right):
    return (left.astype(F32) + right.astype(F32)).astype(left.dtype)


class Reduce:
    def __init__(self, keep, send, axis, order):
        self.keep, self.send, self.axis, self.order = keep, send, axis, list(order)

    def step(self, after=()):
        got = swap(self.send, self.axis, self.order.pop(0))
        got = lax.optimization_barrier((got, after))[0]
        half = self.keep.shape[0] // 2
        if half == 0:
            self.keep, self.send = add_wide(self.keep[0], got[0]), None
        else:
            self.send = add_wide(self.keep[half:], got[half:])
            self.keep = add_wide(self.keep[:half], got[:half])

    def finish(self):
        while self.order:
            self.step()
        return self.keep


def send_direct(keep, send, axis, order):
    half = keep.shape[0]
    pieces = [keep[p] for p in range(half)] + [send[p] for p in range(half)]
    return [
        swap(piece, axis, mask) if mask else piece
        for piece, mask in zip(pieces, places(order))
    ]


class Gather:
    def __init__(self, x, axis, order):
        self.near, self.far, self.axis, self.order = x[None], None, axis, list(order)

    def step(self):
        if self.far is not None:
            self.near = jnp.concatenate([self.near, self.far], axis=0)
        self.far = swap(self.near, self.axis, self.order.pop())

    def finish(self):
        while self.order:
            self.step()
        return self.near, self.far


def hold(x, *chains):
    held = [(c.keep, c.send) if isinstance(c, Reduce) else (c.near, c.far) for c in chains]
    x, held = lax.optimization_barrier((x, held))
    for chain, state in zip(chains, held):
        if isinstance(chain, Reduce):
            chain.keep, chain.send = state
        else:
            chain.near, chain.far = state
    return x


def dot(left, right, dims=NN):
    return lax.dot_general(left, right, (dims, ((), ())), preferred_element_type=F32)


def parts(x, count):
    found = []
    for _ in range(count):
        term = x.astype(BF16)
        found.append(term)
        x = x - term.astype(F32)
    return found


def dot_fine(left, right, dims=NN):
    left_high, left_low = parts(left, 2)
    right_high, right_low = parts(right, 2)
    return (
        dot(left_high, right_high, dims)
        + dot(left_low, right_high, dims)
        + dot(left_high, right_low, dims)
    )


def dot_left(left, right, dims=NN, count=2):
    return sum(dot(term, right, dims) for term in parts(left, count))


def dot_right(left, right, dims=NN, count=2):
    return sum(dot(left, term, dims) for term in parts(right, count))


def silu(x):
    return x * jax.nn.sigmoid(x)


def silu_slope(inputs):
    sigma = jax.nn.sigmoid(inputs)
    return sigma * (1.0 + inputs * (1.0 - sigma))


def softplus(x):
    return jnp.maximum(x, 0.0) + jnp.log1p(jnp.exp(-jnp.abs(x)))


def iota(shape, dim):
    return lax.broadcasted_iota(jnp.int32, shape, dim)


def spread(heads, inner):
    lane, head = iota((heads, inner), 1), iota((heads, inner), 0)
    size = inner // heads
    inside = (lane >= head * size) & (lane < (head + 1) * size)
    return jnp.where(inside, 1.0, 0.0).astype(BF16)


def lane_blocks(heads, inner):
    size = inner // heads
    for start in range(0, inner, LANES):
        stop = min(start + LANES, inner)
        yield start, stop, range(start // size, stop // size)


def head_lanes(start, stop, head, size, length):
    lane = iota((length, stop - start), 1) + start
    return (lane >= head * size) & (lane < (head + 1) * size)


def local(body, outs, args, scratch=(), steps=1, flops=100_000_000):
    def spec(shape, dim, smem=False):
        if smem:
            return pl.BlockSpec(memory_space=pltpu.SMEM)
        block = [size // steps if at == dim else size for at, size in enumerate(shape)]
        return pl.BlockSpec(
            tuple(block),
            lambda step, dim=dim: tuple(step if at == dim else 0 for at in range(len(shape))),
        )

    pairs = [a if isinstance(a, tuple) else (a, None) for a in args]
    trio = [o if len(o) == 3 else (*o, None) for o in outs]
    size = sum(a.size * a.dtype.itemsize for a, _ in pairs)
    return pl.pallas_call(
        body,
        grid=(steps,),
        out_shape=[jax.ShapeDtypeStruct(shape, dtype) for shape, dtype, _ in trio],
        in_specs=[spec(a.shape, dim, a.dtype == jnp.int32) for a, dim in pairs],
        out_specs=[spec(shape, dim) for shape, _, dim in trio],
        scratch_shapes=list(scratch),
        compiler_params=pltpu.CompilerParams(vmem_limit_bytes=60 * 2**20),
        cost_estimate=pl.CostEstimate(
            flops=flops, bytes_accessed=size // 4, transcendentals=0
        ),
    )(*[a for a, _ in pairs])


def accumulate(ref, value):
    first = pl.program_id(0) == 0

    @pl.when(first)
    def _():
        ref[...] = value

    @pl.when(jnp.logical_not(first))
    def _():
        ref[...] += value


def as_row(ref):
    return ref[...].reshape(1, -1)


def as_column(row):
    count = row.shape[1]
    eye = iota((count, count), 0) == iota((count, count), 1)
    return jnp.sum(jnp.where(eye, row, 0.0), axis=1, keepdims=True)


def first_kernel(
    tokens_ref,
    edge_ref,
    gain_ref,
    value_proj_ref,
    state_proj_ref,
    step_proj_ref,
    conv_value_ref,
    conv_value_bias_ref,
    conv_state_ref,
    conv_state_bias_ref,
    step_bias_ref,
    decay_log_ref,
    normed_ref,
    value_in_ref,
    state_in_ref,
    values_ref,
    states_ref,
    value_slope_ref,
    state_slope_ref,
    step_x_ref,
    exp_cum_x_ref,
    end_x_ref,
    weighted_ref,
    cum_ref,
    cum_t_ref,
    step_arg_t_ref,
    ends_ref,
):
    _, length, _ = tokens_ref.shape
    inner = values_ref.shape[2]
    heads = cum_ref.shape[2]
    nstate = states_ref.shape[2] // 2
    blocks, share = ends_ref.shape[0], ends_ref.shape[1] - 8
    spread_mat = spread(heads, inner)
    row, col = iota((length, length), 0), iota((length, length), 1)
    lower = jnp.where(row >= col, 1.0, 0.0).astype(BF16)
    upper = jnp.where(row <= col, 1.0, 0.0).astype(BF16)
    step_bias = as_row(step_bias_ref)
    rate = jnp.exp(as_row(decay_log_ref))
    for source, first, count in ((edge_ref, 0, PAD), (tokens_ref, PAD, length)):
        x = source[0].astype(F32)
        scale = lax.rsqrt(jnp.mean(x * x, axis=-1, keepdims=True) + EPS)
        normed_ref[0, first : first + count] = (x * scale * as_row(gain_ref)).astype(BF16)
    normed = normed_ref[0, PAD:]
    step_arg = dot(normed, step_proj_ref[...], NT) + step_bias
    step_arg_t = dot(step_proj_ref[...], normed, NT) + as_column(step_bias)
    step_arg_t_ref[0] = step_arg_t
    step = softplus(step_arg)
    cum = dot_right(lower, -step * rate, NN, 3)
    cum_ref[0] = cum
    cum_t_ref[0] = dot_left(-softplus(step_arg_t) * as_column(rate), upper, NN, 3)
    step_x = dot_left(step, spread_mat)
    exp_cum_x = dot_left(jnp.exp(cum), spread_mat)
    end_x = dot_left(jnp.exp(cum[length - 1 :] - cum), spread_mat)
    step_x_ref[0] = step_x
    exp_cum_x_ref[0] = exp_cum_x
    end_x_ref[0] = end_x

    def convolve(proj_ref, weight_ref, bias_ref, in_ref, out_ref, slope_ref):
        taps = weight_ref.shape[0]
        in_ref[0] = dot(normed_ref[0], proj_ref[...])
        conv_out = as_row(bias_ref)
        for tap in range(taps):
            first = PAD - taps + 1 + tap
            conv_out = conv_out + weight_ref[tap : tap + 1] * in_ref[0, first : first + length]
        sigma = jax.nn.sigmoid(conv_out)
        slope_ref[0] = sigma * (1.0 + conv_out * (1.0 - sigma))
        out_ref[0] = conv_out * sigma

    convolve(
        state_proj_ref,
        conv_state_ref,
        conv_state_bias_ref,
        state_in_ref,
        states_ref,
        state_slope_ref,
    )
    convolve(
        value_proj_ref,
        conv_value_ref,
        conv_value_bias_ref,
        value_in_ref,
        values_ref,
        value_slope_ref,
    )
    weighted = end_x * step_x * values_ref[0]
    weighted_ref[0] = weighted
    ends = dot_fine(states_ref[0, :, :nstate], weighted, TN)
    for block in range(blocks):
        ends_ref[block, 0:8] = jnp.broadcast_to(exp_cum_x[length - 1 :], (8, inner))
        ends_ref[block, 8:] = ends[block * share : (block + 1) * share]


def scan_kernel(got_ref, entering_ref):
    running = jnp.zeros(entering_ref.shape[1:], F32)
    for block in range(got_ref.shape[0]):
        entering_ref[block] = running
        running = got_ref[block, 0:1] * running + got_ref[block, 8:]


def back_scan_kernel(got_ref, back_ref, leaving_ref):
    running = jnp.zeros(leaving_ref.shape[1:], F32)
    for block in reversed(range(got_ref.shape[0])):
        leaving_ref[block] = running
        running = got_ref[block, 0:1] * running + back_ref[block]


def inside_kernel(
    normed_ref,
    gate_proj_ref,
    values_ref,
    states_ref,
    step_x_ref,
    cum_ref,
    cum_t_ref,
    cot_ref,
    out_proj_ref,
    skip_ref,
    base_ref,
    gnorm_ref,
    gate_pre_ref,
):
    seqs, length, inner = base_ref.shape
    heads = cum_ref.shape[2]
    size = inner // heads
    nstate = states_ref.shape[2] // 2
    skip = dot_left(as_row(skip_ref), spread(heads, inner), NN, 3)
    causal = iota((length, length), 0) >= iota((length, length), 1)
    for seq in range(seqs):
        gate_pre_ref[seq] = dot(normed_ref[seq, PAD:], gate_proj_ref[...])
        products = dot_fine(states_ref[seq, :, nstate:], states_ref[seq, :, :nstate], NT)
        for start, stop, block_heads in lane_blocks(heads, inner):
            values = values_ref[seq, :, start:stop]
            scaled = parts(values * step_x_ref[seq, :, start:stop], 2)
            total = None
            for head in block_heads:
                gap = cum_ref[seq, :, head : head + 1] - cum_t_ref[seq, head : head + 1, :]
                decay = jnp.exp(jnp.where(causal, gap, -1e30))
                high, low = parts(decay * products, 2)
                part = dot(high, scaled[0]) + dot(low, scaled[0]) + dot(high, scaled[1])
                if total is None:
                    total = part
                else:
                    total = jnp.where(head_lanes(start, stop, head, size, length), part, total)
            base_ref[seq, :, start:stop] = total + skip[:, start:stop] * values
        gnorm_ref[seq] = dot(cot_ref[seq * length : (seq + 1) * length], out_proj_ref[...], NT)


def read_kernel(
    state_ref,
    states_ref,
    exp_cum_x_ref,
    base_ref,
    gate_pre_ref,
    gnorm_ref,
    out_gain_ref,
    read_ref,
    sums_ref,
):
    seqs, length, inner = base_ref.shape
    nstate = states_ref.shape[2] // 2
    ones = jnp.ones((8, inner), BF16)
    for seq in range(seqs):
        read = exp_cum_x_ref[seq] * dot_fine(states_ref[seq, :, nstate:], state_ref[seq])
        read_ref[seq] = read
        gated = (base_ref[seq] + read) * silu(gate_pre_ref[seq])
        squares = dot_right(ones, gated * gated, NT)
        backs = dot_right(ones, gnorm_ref[seq] * as_row(out_gain_ref) * gated, NT)
        row = iota((8, length), 0)
        sums_ref[:, seq * length : (seq + 1) * length] = jnp.where(row == 0, squares, backs)


def gate_kernel(
    sums_ref,
    read_ref,
    base_ref,
    gate_pre_ref,
    gnorm_ref,
    out_gain_ref,
    exp_cum_x_ref,
    states_ref,
    grad_scan_ref,
    back_ref,
    *,
    inner_total,
):
    nstate = states_ref.shape[2] // 2
    blocks, share = back_ref.shape[0], back_ref.shape[1]
    sums = jnp.transpose(sums_ref[...])
    scale = lax.rsqrt(sums[:, 0:1] / inner_total + EPS)
    back_mean = scale * sums[:, 1:2] / inner_total
    gate_act = silu(gate_pre_ref[0])
    unit = (base_ref[0] + read_ref[0]) * gate_act * scale
    grad_gated = scale * (gnorm_ref[0] * as_row(out_gain_ref) - unit * back_mean)
    grad_scan = grad_gated * gate_act
    grad_scan_ref[0] = grad_scan
    back = dot_fine(states_ref[0, :, nstate:], exp_cum_x_ref[0] * grad_scan, TN)
    for block in range(blocks):
        back_ref[block] = back[block * share : (block + 1) * share]


def cut_lines(held, value):
    count = held.shape[1]
    for piece in range(held.shape[0]):
        held[piece] = value[piece * count : (piece + 1) * count]


def stacked(lines, lanes):
    return [lines[:, at : at + lanes] for at in range(0, lines.shape[1], lanes)]


def ordered_piece(own, at, value, keep_ref, send_ref):
    half = keep_ref.shape[0]
    for p, mask in enumerate(places(orders(2 * half)[0])):

        @pl.when((own ^ mask) == at)
        def _():
            (keep_ref if p < half else send_ref)[p % half, :, : value.shape[1]] = value


def low_kernel(
    own_ref,
    sums_ref,
    read_ref,
    base_ref,
    gate_pre_ref,
    gnorm_ref,
    out_gain_ref,
    grad_scan_ref,
    values_ref,
    normed_ref,
    cot_ref,
    out_proj_ref,
    proj_ref,
    grad_gate_ref,
    rows_ref,
    gain_row_ref,
    keep_ref,
    send_ref,
    branch_keep_ref,
    branch_send_ref,
    gate_low,
    grad_gate_proj,
    grad_out_proj,
    *,
    inner_total,
):
    seqs, length, inner = base_ref.shape
    gain_sum = jnp.zeros((1, inner), F32)
    skip_sum = jnp.zeros((1, inner), F32)
    pieces = 2 * branch_keep_ref.shape[0]
    col_width = branch_keep_ref.shape[2]
    total = None
    for seq in range(seqs):
        sums = jnp.transpose(sums_ref[:, seq * length : (seq + 1) * length])
        scale = lax.rsqrt(sums[:, 0:1] / inner_total + EPS)
        back_mean = scale * sums[:, 1:2] / inner_total
        gate_pre = gate_pre_ref[seq]
        sigma = jax.nn.sigmoid(gate_pre)
        scan_out = base_ref[seq] + read_ref[seq]
        unit = scan_out * gate_pre * sigma * scale
        gnorm = gnorm_ref[seq]
        gate_low[seq * length : (seq + 1) * length] = (unit * as_row(out_gain_ref)).astype(BF16)
        grad_gated = scale * (gnorm * as_row(out_gain_ref) - unit * back_mean)
        slope = sigma * (1.0 + gate_pre * (1.0 - sigma))
        grad_gate = (grad_gated * scan_out * slope).astype(BF16)
        grad_gate_ref[seq] = grad_gate
        part = dot(normed_ref[seq, PAD:], grad_gate, TN)
        total = part if total is None else total + part
        gain_sum = gain_sum + jnp.sum(gnorm * unit, axis=0, keepdims=True)
        skip_sum = skip_sum + jnp.sum(
            grad_scan_ref[seq] * values_ref[seq], axis=0, keepdims=True
        )
    rows_ref[:, :inner] = gain_sum
    rows_ref[:, inner:] = skip_sum
    ones = jnp.ones((8, inner), BF16)
    gain_row_ref[...] = dot_right(ones, total * proj_ref[...].astype(F32), NT)
    cut_lines(grad_gate_proj, total)
    cut_lines(grad_out_proj, dot(gate_low[...], cot_ref[...], TN))
    blocks = 2 * keep_ref.shape[0]
    for p, mask in enumerate(places(orders(blocks)[0])):
        at = own_ref[0] ^ mask
        ref = keep_ref if p < blocks // 2 else send_ref
        value = jnp.concatenate(
            [grad_gate_proj[at], *stacked(grad_out_proj[at], inner)], axis=0
        )
        ref[p % (blocks // 2)] = value.astype(BF16)
    branch = dot(gate_low[...], out_proj_ref[...])
    for piece in range(pieces):
        value = branch[:, piece * col_width : (piece + 1) * col_width].astype(BF16)
        ordered_piece(own_ref[1], piece, value, branch_keep_ref, branch_send_ref)


def mix_kernel(
    values_ref,
    states_ref,
    step_x_ref,
    exp_cum_x_ref,
    cum_ref,
    cum_t_ref,
    grad_scan_ref,
    state_ref,
    scaled_grad_ref,
    grad_b_ref,
    grad_c_ref,
    gaps_ref,
):
    seqs, length, inner = grad_scan_ref.shape
    heads = cum_ref.shape[2]
    size = inner // heads
    nstate = states_ref.shape[2] // 2
    causal = iota((length, length), 0) >= iota((length, length), 1)
    ones = jnp.ones((8, length), BF16)
    for seq in range(seqs):
        b_rows = states_ref[seq, :, :nstate]
        c_rows = states_ref[seq, :, nstate:]
        products = dot_fine(c_rows, b_rows, NT)
        grad_products = jnp.zeros((length, length), F32)
        for start, stop, block_heads in lane_blocks(heads, inner):
            scaled = values_ref[seq, :, start:stop] * step_x_ref[seq, :, start:stop]
            scaled_high, scaled_low = parts(scaled, 2)
            scan_high, scan_low = parts(grad_scan_ref[seq, :, start:stop], 2)
            total = None
            for head in block_heads:
                gap = cum_ref[seq, :, head : head + 1] - cum_t_ref[seq, head : head + 1, :]
                decay = jnp.exp(jnp.where(causal, gap, -1e30))
                own = head_lanes(start, stop, head, size, length)
                own_high = jnp.where(own, scan_high, jnp.zeros_like(scan_high))
                own_low = jnp.where(own, scan_low, jnp.zeros_like(scan_low))
                grad_mix = (
                    dot(own_high, scaled_high, NT)
                    + dot(own_low, scaled_high, NT)
                    + dot(own_high, scaled_low, NT)
                )
                grad_decayed = grad_mix * decay
                grad_products = grad_products + grad_decayed
                related = (grad_decayed * products).astype(BF16)
                gaps = dot(ones, related, NT) - dot(ones, related)
                gaps_ref[seq, head : head + 1] = gaps[0:1]
                part = dot((decay * products).astype(BF16), own_high, TN)
                total = part if total is None else total + part
            scaled_grad_ref[seq, :, start:stop] = total
        carried = exp_cum_x_ref[seq] * grad_scan_ref[seq]
        grad_c_ref[seq] = dot_fine(grad_products, b_rows) + dot_fine(
            carried, state_ref[seq], NT
        )
        grad_b_ref[seq] = dot_fine(grad_products, c_rows, TN)


def state_sum_kernel(
    own_ref,
    grad_end_ref,
    weighted_ref,
    grad_b_ref,
    grad_c_ref,
    keep_ref,
    send_ref,
):
    pieces, part = 2 * keep_ref.shape[0], keep_ref.shape[2]
    grad_b = grad_b_ref[0] + dot_fine(weighted_ref[0], grad_end_ref[0], NT)
    both = jnp.concatenate([grad_b, grad_c_ref[0]], axis=1)
    for piece in range(pieces):
        value = both[:, piece * part : (piece + 1) * part]
        ordered_piece(own_ref[1], piece, value, keep_ref, send_ref)


def conv_back(grad_out, in_ref, weight_ref, seq, around):
    length = grad_out.shape[0]
    taps = weight_ref.shape[0]
    around[PAD : PAD + length] = grad_out
    grad_in = None
    sums = []
    for tap in range(taps):
        first = PAD - taps + 1 + tap
        sums.append(
            jnp.sum(grad_out * in_ref[seq, first : first + length], axis=0, keepdims=True)
        )
        first = taps - 1 - tap
        part = weight_ref[tap : tap + 1] * around[first : first + PAD + length]
        grad_in = part if grad_in is None else grad_in + part
    sums.append(jnp.sum(grad_out, axis=0, keepdims=True))
    return grad_in, jnp.concatenate(sums, axis=0)


def clear_edges(around):
    zeros = jnp.zeros((PAD, around.shape[1]), F32)
    around[0:PAD] = zeros
    around[around.shape[0] - PAD :] = zeros


def value_kernel(
    grad_end_ref,
    state_ref,
    values_ref,
    states_ref,
    slope_ref,
    conv_in_ref,
    conv_weight_ref,
    step_x_ref,
    exp_cum_x_ref,
    end_x_ref,
    step_arg_t_ref,
    decay_log_ref,
    skip_ref,
    read_ref,
    grad_scan_ref,
    scaled_grad_ref,
    gaps_ref,
    grad_in_ref,
    grad_step_t_ref,
    conv_rows_ref,
    head_rows_ref,
    around,
):
    _, length, inner = values_ref.shape
    heads = gaps_ref.shape[1]
    nstate = states_ref.shape[2] // 2
    spread_mat = spread(heads, inner)
    row, col = iota((length, length), 0), iota((length, length), 1)
    lower = jnp.where(row >= col, 1.0, 0.0).astype(BF16)
    rate_t = as_column(jnp.exp(as_row(decay_log_ref)))
    skip = dot_left(as_row(skip_ref), spread_mat, NN, 3)
    last = iota((heads, length), 1) == length - 1
    clear_edges(around)
    values = values_ref[0]
    grad_end = grad_end_ref[0]
    step_x = step_x_ref[0]
    grad_scan = grad_scan_ref[0]
    end_proj = end_x_ref[0] * dot(
        states_ref[0, :, :nstate].astype(BF16), grad_end.astype(BF16)
    )
    scaled_grad = scaled_grad_ref[0] + end_proj
    grad_in, conv_rows = conv_back(
        (skip * grad_scan + step_x * scaled_grad) * slope_ref[0],
        conv_in_ref,
        conv_weight_ref,
        0,
        around,
    )
    grad_in_ref[0] = grad_in
    end_terms = dot_right(spread_mat, step_x * values * end_proj, NT)
    crossed = jnp.sum(grad_end * state_ref[0], axis=0, keepdims=True)
    crossed = crossed * exp_cum_x_ref[0, length - 1 :]
    last_term = jnp.sum(end_terms, axis=1, keepdims=True) + jnp.sum(
        jnp.where(spread_mat.astype(F32) > 0.0, crossed, 0.0), axis=1, keepdims=True
    )
    grad_cum = (
        gaps_ref[0] + dot_right(spread_mat, grad_scan * read_ref[0], NT) - end_terms
    ) + jnp.where(last, last_term, 0.0)
    grad_log = dot_left(grad_cum, lower, NN, 3)
    step_arg = step_arg_t_ref[0]
    rate_sum = -jnp.sum(grad_log * softplus(step_arg), axis=1, keepdims=True)
    grad_step = dot_right(spread_mat, values * scaled_grad, NT) - grad_log * rate_t
    grad_step = grad_step * jax.nn.sigmoid(step_arg)
    bias_sum = jnp.sum(grad_step, axis=1, keepdims=True)
    grad_step_t_ref[0] = grad_step.astype(BF16)
    lane = iota((heads, LANES), 1)
    accumulate(conv_rows_ref, conv_rows)
    accumulate(head_rows_ref, jnp.where(lane == 0, bias_sum, rate_sum * rate_t))


def small_places(heads, taps, lanes):
    return lanes - LANES, heads + max(heads, taps)


def weight_kernel(
    own_ref,
    normed_ref,
    value_in_ref,
    grad_step_t_ref,
    state_grad_ref,
    slope_ref,
    conv_in_ref,
    conv_weight_ref,
    gain_ref,
    gate_gain_row_ref,
    value_proj_ref,
    state_proj_t_ref,
    step_proj_t_ref,
    value_rows_ref,
    head_rows_ref,
    inner_row_ref,
    state_in_ref,
    keep_ref,
    send_ref,
    around,
    small,
    slope,
    conv_in,
    conv_weight,
    late,
    *,
    pieces,
):
    seqs, length, part = slope.shape
    for piece in range(pieces):

        @pl.when(own_ref[1] == piece)
        def _():
            lanes = slice(piece * part, (piece + 1) * part)
            slope[...] = slope_ref[:, :, lanes]
            conv_in[...] = conv_in_ref[:, :, lanes]
            conv_weight[...] = conv_weight_ref[:, lanes]

    width = normed_ref.shape[2]
    blocks, _, inner = late.shape
    value_total = state_total = step_total = conv_total = None

    def add(total, part):
        return part if total is None else total + part

    clear_edges(around)
    for seq in range(seqs):
        normed = normed_ref[seq]
        grad = state_grad_ref[seq * length : (seq + 1) * length] * slope[seq]
        grad_in, conv_rows = conv_back(grad, conv_in, conv_weight, seq, around)
        state_in_ref[seq] = grad_in
        conv_total = add(conv_total, conv_rows)
        value_total = add(value_total, dot(normed, value_in_ref[seq].astype(BF16), TN))
        state_total = add(state_total, dot(grad_in.astype(BF16), normed, TN))
        step_total = add(step_total, dot(grad_step_t_ref[seq], normed_ref[seq, PAD:]))
    ones = jnp.ones((8, inner), BF16)
    gain_row = gate_gain_row_ref[...] + dot_right(
        ones, value_total * value_proj_ref[...].astype(F32), NT
    )
    gain_row = (
        gain_row[0:1]
        + jnp.sum(state_total * state_proj_t_ref[...].astype(F32), axis=0, keepdims=True)
        + jnp.sum(step_total * step_proj_t_ref[...].astype(F32), axis=0, keepdims=True)
    )
    heads, taps = step_total.shape[0], value_rows_ref.shape[0]
    heads_at, last = small_places(heads, taps, small.shape[1])
    small[...] = jnp.zeros(small.shape, F32)
    small[:heads, :width] = step_total
    small[heads : heads + taps, :inner] = value_rows_ref[...]
    for piece in range(pieces):

        @pl.when(own_ref[1] == piece)
        def _():
            first = inner + piece * part
            small[heads : heads + taps, first : first + part] = conv_total

    small[heads : 2 * heads, heads_at:] = head_rows_ref[...]
    small[last : last + 1, : 2 * inner] = inner_row_ref[...]
    small[last + 1 : last + 2, :width] = gain_row / as_row(gain_ref)
    small_rows = jnp.concatenate(stacked(small[...], inner), axis=0)
    small_lines = small_rows.shape[0] // blocks
    value_lines = width // blocks
    state_lines = state_total.shape[0] // blocks
    for block in range(blocks):
        value = value_total[block * value_lines : (block + 1) * value_lines]
        state = state_total[block * state_lines : (block + 1) * state_lines]
        lines = small_rows[block * small_lines : (block + 1) * small_lines]
        value = [value, *stacked(state, inner), *[x.astype(F32) for x in parts(lines, 2)]]
        spare = late.shape[1] - sum(x.shape[0] for x in value)
        if spare:
            value.append(jnp.zeros((spare, inner), F32))
        late[block] = jnp.concatenate(value, axis=0).astype(BF16)
    for p, mask in enumerate(places(orders(blocks)[0])):
        ref = keep_ref if p < blocks // 2 else send_ref
        ref[p % (blocks // 2)] = late[own_ref[0] ^ mask]


def sum_terms(terms, first, lines):
    total = terms[0].astype(F32)
    for term in terms[1:]:
        total = total + term.astype(F32)
    small = total[first : first + lines] + total[first + lines : first + 2 * lines]
    small = [x.astype(F32) for x in parts(small, 2)]
    spare = [total[first + 2 * lines :]] if total.shape[0] > first + 2 * lines else []
    return jnp.concatenate([total[:first], *small, *spare], axis=0).astype(BF16)


def pair_kernel(keep_ref, got_ref, *out_refs, **small):
    for block, out_ref in enumerate(out_refs):
        out_ref[...] = sum_terms([keep_ref[block], got_ref[block]], **small)


def sum_kernel(*refs, **small):
    total = sum_terms([ref[...] for ref in refs[:-1]], **small)
    for block in range(refs[-1].shape[0]):
        refs[-1][block] = total


def place_kernel(own_ref, near_ref, far_ref, gate_ref, out_ref):
    blocks, lines, inner = gate_ref.shape
    count = out_ref.shape[1]
    for p, mask in enumerate(places(orders(blocks)[0])):
        ref = near_ref if p < blocks // 2 else far_ref
        value = ref[p % (blocks // 2)].astype(F32)
        at = own_ref[0] ^ mask
        gate_ref[at] = value[:lines]
        for group in range(out_ref.shape[2] // inner):
            first = lines + group * count
            out_ref[at, :, group * inner : (group + 1) * inner] = value[first : first + count]


def back_kernel(
    own_ref,
    tokens_ref,
    gain_ref,
    value_in_ref,
    state_in_ref,
    value_over_ref,
    state_over_ref,
    value_proj_ref,
    state_proj_t_ref,
    grad_gate_ref,
    gate_proj_ref,
    grad_step_t_ref,
    step_proj_t_ref,
    keep_ref,
    send_ref,
    *,
    col_width,
):
    _, length, width = tokens_ref.shape
    pieces = 2 * keep_ref.shape[0]
    def whole(in_ref, over_ref, seq):
        return jnp.concatenate(
            [
                in_ref[seq, PAD:length].astype(BF16),
                (in_ref[seq, length:] + over_ref[seq]).astype(BF16),
            ],
            axis=0,
        )

    x = tokens_ref[0].astype(F32)
    unit = x * lax.rsqrt(jnp.mean(x * x, axis=-1, keepdims=True) + EPS)
    normed_grad = (
        dot(whole(value_in_ref, value_over_ref, 0), value_proj_ref[...], NT)
        + dot(whole(state_in_ref, state_over_ref, 0), state_proj_t_ref[...])
        + dot(grad_gate_ref[0], gate_proj_ref[...], NT)
        + dot(grad_step_t_ref[0], step_proj_t_ref[...], TN)
    )
    unit_grad = normed_grad * as_row(gain_ref)
    row_sum = jnp.sum(unit_grad * unit, axis=-1, keepdims=True).astype(BF16)
    row_sum = jnp.broadcast_to(row_sum, (length, LANES))
    for half_ref in (keep_ref, send_ref):
        for p in range(pieces // 2):
            half_ref[p, :, half_ref.shape[2] - LANES :] = row_sum
    for piece in range(pieces):
        value = unit_grad[:, piece * col_width : (piece + 1) * col_width].astype(BF16)
        ordered_piece(own_ref[1], piece, value, keep_ref, send_ref)


def last_kernel(
    own_ref,
    near_ref,
    far_ref,
    state_proj_ref,
    norm_gain_ref,
    step_proj_ref,
    conv_value_ref,
    conv_value_bias_ref,
    conv_state_ref,
    conv_state_bias_ref,
    step_bias_ref,
    decay_log_ref,
    skip_gain_ref,
    out_gain_ref,
    held,
    smalls,
):
    half, blocks, _, inner = near_ref.shape
    pieces, _, each, width = held.shape
    _, lines, lanes = smalls.shape
    state_lines = each * width // inner
    small_lines = lines * lanes // inner // blocks
    for p, mask in enumerate(places(orders(2 * half)[0])):
        ref = near_ref if p < half else far_ref
        at = own_ref[1] ^ mask
        small = []
        for block in range(blocks):
            value = ref[p % half, block].astype(F32)
            for group in range(width // inner):
                held[at, block, :, group * inner : (group + 1) * inner] = value[
                    group * each : (group + 1) * each
                ]
            high = value[state_lines : state_lines + small_lines]
            small.append(high + value[state_lines + small_lines : state_lines + 2 * small_lines])
        small = jnp.concatenate(small, axis=0)
        smalls[at] = jnp.concatenate(
            [small[first : first + lines] for first in range(0, small.shape[0], lines)], axis=1
        )
    state_proj_ref[...] = jnp.transpose(held[...].reshape(-1, width))
    whole = smalls[0]
    for piece in range(1, pieces):
        whole = whole + smalls[piece]
    small = smalls[own_ref[1]]
    heads = step_proj_ref.shape[0]
    taps = conv_value_ref.shape[0]
    channels = inner + conv_state_ref.shape[1]
    heads_at, last = small_places(heads, taps + 1, lanes)
    norm_gain_ref[...] = whole[last + 1, :width]
    step_proj_ref[...] = small[:heads, :width]
    conv_value_ref[...] = small[heads : heads + taps, :inner]
    conv_value_bias_ref[...] = small[heads + taps, :inner]
    conv_state_ref[...] = whole[heads : heads + taps, inner:channels]
    conv_state_bias_ref[...] = whole[heads + taps, inner:channels]
    sums = small[heads : 2 * heads, heads_at : heads_at + 2]
    eye = iota((heads, heads), 0) == iota((heads, heads), 1)
    step_bias_ref[...] = jnp.sum(jnp.where(eye, sums[:, 0:1], 0.0), axis=0)
    decay_log_ref[...] = jnp.sum(jnp.where(eye, sums[:, 1:2], 0.0), axis=0)
    row = small[last : last + 1, : 2 * inner]
    out_gain_ref[...] = row[0, :inner]
    skip = dot_left(row[:, inner:], spread(heads, inner), NT, 3)
    skip_gain_ref[...] = skip.reshape(heads)


def on_device(
    tokens,
    norm_gain,
    gate_proj,
    value_proj,
    state_proj,
    step_proj,
    conv_value,
    conv_value_bias,
    conv_state,
    conv_state_bias,
    step_bias,
    decay_log,
    skip_gain,
    out_gain,
    out_proj,
    cotangent,
):
    seqs, length, width = tokens.shape
    rows = seqs * length
    heads = step_proj.shape[1]
    inner = gate_proj.shape[1]
    head_dim = inner // heads
    nstate = state_proj.shape[1] // 2
    taps = conv_value.shape[0]
    channels = inner + 2 * nstate
    head_devices = lax.axis_size("head")
    blocks = lax.axis_size("seq")
    head_index = lax.axis_index("head")
    own = jnp.stack([lax.axis_index("seq"), head_index]).astype(jnp.int32)
    col_width = width // head_devices
    share = seqs * nstate // blocks
    part = 2 * nstate // head_devices
    full = (seqs, length, inner)
    inner_total = inner * head_devices

    def own_cols(x, size):
        return lax.dynamic_slice_in_dim(x, head_index * size, size, x.ndim - 1)

    def cut(*arrays):
        return [(x, 0) for x in arrays]

    edge_tokens = shift(tokens[:, length - PAD :, :], "seq", 1)
    step_proj_t = jnp.transpose(step_proj)
    state_proj_t = jnp.transpose(state_proj)
    state_proj_t = lax.dynamic_slice_in_dim(state_proj_t, head_index * part, part, 0)
    (
        normed,
        value_conv_in,
        state_conv_in,
        values,
        states,
        value_slope,
        state_slope,
        step_x,
        exp_cum_x,
        end_x,
        weighted,
        cum,
        cum_t,
        step_arg_t,
        ends,
    ) = local(
        first_kernel,
        [
            ((seqs, PAD + length, width), BF16, 0),
            ((seqs, PAD + length, inner), F32, 0),
            ((seqs, PAD + length, 2 * nstate), F32, 0),
            (full, F32, 0),
            ((seqs, length, 2 * nstate), F32, 0),
            (full, F32, 0),
            ((seqs, length, 2 * nstate), F32, 0),
            (full, F32, 0),
            (full, F32, 0),
            (full, F32, 0),
            (full, F32, 0),
            ((seqs, length, heads), F32, 0),
            ((seqs, heads, length), F32, 0),
            ((seqs, heads, length), F32, 0),
            ((blocks, 8 + share, inner), F32, 0),
        ],
        [
            *cut(tokens, edge_tokens),
            norm_gain,
            value_proj,
            state_proj,
            step_proj_t,
            conv_value,
            conv_value_bias,
            conv_state,
            conv_state_bias,
            step_bias,
            decay_log,
        ],
        steps=seqs,
    )
    got = lax.all_to_all(ends, "seq", 0, 0)
    cot_rows = cotangent.reshape(rows, col_width)
    cot_low, _ = lax.optimization_barrier((cot_rows.astype(BF16), ends))
    cot_low = lax.all_gather(cot_low, "head", axis=1, tiled=True)
    got, cot_low = lax.optimization_barrier((got, cot_low))
    (entering,) = local(scan_kernel, [((blocks, share, inner), F32)], [got])
    state_in = lax.all_to_all(entering, "seq", 0, 0).reshape(seqs, nstate, inner)
    base, gnorm, gate_pre = local(
        inside_kernel,
        [(full, F32, 0), (full, F32, 0), (full, F32, 0)],
        [
            (normed, 0),
            gate_proj,
            *cut(values, states, step_x, cum, cum_t, cot_low),
            out_proj,
            skip_gain,
        ],
        steps=seqs,
    )
    read, row_sums = local(
        read_kernel,
        [(full, F32, 0), ((8, rows), F32, 1)],
        [*cut(state_in, states, exp_cum_x, base, gate_pre, gnorm), out_gain],
        steps=seqs,
    )
    row_sums = sum_all(row_sums, "head")
    grad_scan, back = local(
        functools.partial(gate_kernel, inner_total=inner_total),
        [(full, F32, 0), ((blocks, share, inner), F32, 0)],
        [
            (row_sums, 1),
            *cut(read, base, gate_pre, gnorm),
            out_gain,
            *cut(exp_cum_x, states),
        ],
        steps=seqs,
    )
    got_back = lax.all_to_all(back, "seq", 0, 0)

    def halves(axis_size, lines, lanes, dtype=BF16, dim=None):
        return [((axis_size // 2, lines, lanes), dtype, dim)] * 2

    (
        grad_gate,
        inner_row,
        gate_gain_row,
        early_keep,
        early_send,
        branch_keep,
        branch_send,
    ) = local(
        functools.partial(low_kernel, inner_total=inner_total),
        [
            (full, BF16),
            ((1, 2 * inner), F32),
            ((8, width), F32),
            *halves(blocks, 2 * (width // blocks), inner),
            *halves(head_devices, rows, col_width),
        ],
        [
            own,
            row_sums,
            read,
            base,
            gate_pre,
            gnorm,
            out_gain,
            grad_scan,
            values,
            normed,
            cot_low,
            out_proj,
            gate_proj,
        ],
        [
            pltpu.VMEM((rows, inner), BF16),
            pltpu.VMEM((blocks, width // blocks, inner), F32),
            pltpu.VMEM((blocks, inner // blocks, width), F32),
        ],
    )

    got_back = lax.optimization_barrier((got_back, early_send))[0]
    (leaving,) = local(back_scan_kernel, [((blocks, share, inner), F32)], [got, got_back])
    grad_end = lax.all_to_all(leaving, "seq", 0, 0).reshape(seqs, nstate, inner)
    near = orders(blocks)[0]
    near_head = orders(head_devices)[0]
    even = places(near)[: blocks // 2]
    branch_chain = Reduce(branch_keep, branch_send, "head", near_head)
    grad_scan = lax.optimization_barrier((grad_scan, leaving))[0]
    scaled_grad, grad_b, grad_c, gaps = local(
        mix_kernel,
        [
            (full, F32, 0),
            ((seqs, length, nstate), F32, 0),
            ((seqs, length, nstate), F32, 0),
            ((seqs, heads, length), F32, 0),
        ],
        cut(values, states, step_x, exp_cum_x, cum, cum_t, grad_scan, state_in),
        steps=seqs,
    )
    early = lax.optimization_barrier((swap(early_send, "seq", 1), gaps))[0]
    early = add_wide(early_keep, early)
    grad_end, early = lax.optimization_barrier((grad_end, early))
    early = [
        swap(early[p], "seq", mask) if mask else early[p] for p, mask in enumerate(even)
    ]
    state_keep, state_send = local(
        state_sum_kernel,
        halves(head_devices, rows, part, F32, 1),
        [own, *cut(grad_end, weighted, grad_b, grad_c)],
        steps=seqs,
    )
    state_part = send_direct(state_keep, state_send, "head", near_head)
    state_part = sum(state_part[1:], state_part[0])
    value_in, grad_step_t, value_rows, head_rows = local(
        value_kernel,
        [
            ((seqs, PAD + length, inner), F32, 0),
            ((seqs, heads, length), BF16, 0),
            ((taps + 1, inner), F32),
            ((heads, LANES), F32),
        ],
        [
            *cut(grad_end, state_in, values, states, value_slope, value_conv_in),
            conv_value,
            *cut(step_x, exp_cum_x, end_x, step_arg_t),
            decay_log,
            skip_gain,
            *cut(read, grad_scan, scaled_grad, gaps),
        ],
        [pltpu.VMEM((length + 2 * PAD, inner), F32)],
        steps=seqs,
    )
    value_lines = width // blocks
    state_lines = part // blocks * (width // inner)
    small_lanes = max(width, channels + LANES)
    small_rows = -(-(heads + max(heads, taps + 1) + 2) // 8) * 8
    small_lines = small_rows * (small_lanes // inner) // blocks
    late_lines = -(-(value_lines + state_lines + 2 * small_lines) // 16) * 16
    state_grad_in, late_keep, late_send = local(
        functools.partial(weight_kernel, pieces=head_devices),
        [
            ((seqs, PAD + length, part), F32),
            *halves(blocks, late_lines, inner),
        ],
        [
            own,
            normed,
            value_in,
            grad_step_t,
            state_part,
            state_slope,
            state_conv_in,
            conv_state,
            norm_gain,
            gate_gain_row,
            value_proj,
            state_proj_t,
            step_proj_t,
            value_rows,
            head_rows,
            inner_row,
        ],
        [
            pltpu.VMEM((length + 2 * PAD, part), F32),
            pltpu.VMEM((small_rows, small_lanes), F32),
            pltpu.VMEM((seqs, length, part), F32),
            pltpu.VMEM((seqs, PAD + length, part), F32),
            pltpu.VMEM((taps, part), F32),
            pltpu.VMEM((blocks, late_lines, inner), BF16),
        ],
    )
    late_send, early = lax.optimization_barrier((late_send, early))
    late = swap(late_send, "seq", 1)
    early = sum(x.astype(F32) for x in early).astype(BF16)
    early = [swap(early, "seq", mask) if mask else early for mask in even]
    late_small = dict(first=value_lines + state_lines, lines=small_lines)
    late = local(
        functools.partial(pair_kernel, **late_small),
        [((late_lines, inner), BF16)] * (blocks // 2),
        [late_keep, late],
    )
    late = [swap(x, "seq", mask) if mask else x for x, mask in zip(late, even)]
    over = jnp.concatenate([value_in[:, :PAD], state_grad_in[:, :PAD]], axis=2)
    over = shift(over, "seq", -1)
    own_source = own_cols(tokens.reshape(rows, width), col_width).astype(F32)
    back_width = -(-(col_width + 1) // LANES) * LANES
    keep, send = local(
        functools.partial(back_kernel, col_width=col_width),
        [
            *halves(head_devices, rows, back_width, BF16, 1),
        ],
        [
            own,
            (tokens, 0),
            norm_gain,
            *cut(value_in, state_grad_in, over[:, :, :inner], over[:, :, inner:]),
            value_proj,
            state_proj_t,
            (grad_gate, 0),
            gate_proj,
            (grad_step_t, 0),
            step_proj_t,
        ],
        steps=seqs,
    )
    branch_chain.step()
    branch_chain.step(after=(keep,))
    branch = branch_chain.finish().astype(F32)
    mixed_rows = jnp.swapaxes((own_source + branch).reshape(seqs, length, col_width), 1, 2)
    early = jnp.stack(early)
    late, mixed_rows, early, keep, send = lax.optimization_barrier(
        (late, mixed_rows, early, keep, send)
    )
    early_far = swap(early, "seq", 1)
    (late_values,) = local(
        functools.partial(sum_kernel, **late_small),
        [((blocks, late_lines, inner), BF16)],
        late,
    )
    late = lax.all_to_all(late_values, "seq", 0, 0)
    own_part = send_direct(keep, send, "head", near_head)
    own_part = sum(x.astype(F32) for x in own_part)
    row_mean = own_part[:, back_width - 1 :] / width
    own_part = own_part[:, :col_width]
    source = tokens.reshape(rows, width).astype(F32)
    own_scale = lax.rsqrt(jnp.mean(source * source, axis=-1, keepdims=True) + EPS)
    own_unit = own_source * own_scale
    grad_tokens = cot_rows + own_scale * (own_part - own_unit * row_mean)
    grad_tokens = jnp.swapaxes(grad_tokens.reshape(seqs, length, col_width), 1, 2)
    late, grad_tokens = lax.optimization_barrier((late, grad_tokens))
    grad_value_proj = late[:, :value_lines].reshape(width, inner).astype(F32)
    grad_gate_proj, grad_out_proj = local(
        place_kernel,
        [
            ((blocks, value_lines, inner), F32),
            ((blocks, inner // blocks, width), F32),
        ],
        [own, early, early_far],
    )
    grad_gate_proj = grad_gate_proj.reshape(width, inner)
    grad_out_proj = grad_out_proj.reshape(inner, width)
    state_chain = Gather(late[:, value_lines:], "head", near_head)
    state_chain.step()
    done = (grad_gate_proj, grad_out_proj, mixed_rows, grad_tokens)
    grad_gate_proj, grad_out_proj, mixed_rows, grad_tokens = hold(done, state_chain)
    (
        grad_state_proj,
        grad_norm_gain,
        grad_step_proj,
        grad_conv_value,
        grad_conv_value_bias,
        grad_conv_state,
        grad_conv_state_bias,
        grad_step_bias,
        grad_decay_log,
        grad_skip_gain,
        grad_out_gain,
    ) = local(
        last_kernel,
        [
            ((width, 2 * nstate), F32),
            ((width,), F32),
            ((heads, width), F32),
            ((taps, inner), F32),
            ((inner,), F32),
            ((taps, 2 * nstate), F32),
            ((2 * nstate,), F32),
            ((heads,), F32),
            ((heads,), F32),
            ((heads,), F32),
            ((inner,), F32),
        ],
        [own, *state_chain.finish()],
        [
            pltpu.VMEM((head_devices, blocks, part // blocks, width), F32),
            pltpu.VMEM((head_devices, small_rows, small_lanes), F32),
        ],
    )
    return (
        jnp.swapaxes(mixed_rows, 1, 2),
        jnp.swapaxes(grad_tokens, 1, 2),
        grad_norm_gain,
        grad_gate_proj,
        grad_value_proj,
        grad_state_proj,
        jnp.transpose(grad_step_proj),
        grad_conv_value,
        grad_conv_value_bias,
        grad_conv_state,
        grad_conv_state_bias,
        grad_step_bias,
        grad_decay_log,
        grad_skip_gain,
        grad_out_gain,
        grad_out_proj,
    )


def solution(mesh):
    return jax.shard_map(
        on_device,
        mesh=mesh,
        in_specs=(
            P(None, "seq", None),
            P(),
            P(None, "head"),
            P(None, "head"),
            P(),
            P(None, "head"),
            P(None, "head"),
            P("head"),
            P(),
            P(),
            P("head"),
            P("head"),
            P("head"),
            P("head"),
            P("head", None),
            P(None, "seq", "head"),
        ),
        out_specs=(
            P(None, "seq", "head"),
            P(None, "seq", "head"),
            P(),
            P(None, "head"),
            P(None, "head"),
            P(),
            P(None, "head"),
            P(None, "head"),
            P("head"),
            P(),
            P(),
            P("head"),
            P("head"),
            P("head"),
            P("head"),
            P("head", None),
        ),
        check_vma=False,
    )
```
